256 devices in a mesh: row: 8 (over y, z_lo), col: 32 (over x, z_hi, core).
Axes of the slice: x: 4, y: 4, z: 8 (z_hi: 4, z_lo: 2; z = z_hi * 2 + z_lo), core: 2. Of those that a mesh axis runs over, the one named last changes fastest.
Arguments:
- velocity: bfloat16 [3, 512, 1024, 256], P(None, 'row', 'col'), may hold values from -6 to 6
- adj_temp: bfloat16 [512, 1024, 256], P('row', 'col'), may hold values from -6 to 6
- radial_div: bfloat16 [256, 256], replicated, may hold values from -0.375 to 0.375
- reciprocal_distance: float32 [256], replicated, may hold values from 0.002 to 0.02
- radial_basis: bfloat16 [168, 256, 256], P('row'), may hold values from -0.375 to 0.375
- radial_eig: float32 [168, 256], P('row'), may hold values from 0.5 to 8
- axial_diff: bfloat16 [1024, 1024], replicated, may hold values from -0.1875 to 0.1875
- axial_basis: bfloat16 [1024, 1024], replicated, may hold values from -0.1875 to 0.1875
- axial_eig: float32 [1024], replicated, may hold values from 0.5 to 8
Outputs:
- new_temp: float32 [168, 2, 1024, 256], P('row', None, 'col')
The draws below stay inside these ranges and needn't reach their ends.
All inputs are finite; a program needn't handle non-finite values.
Results may differ from the reference program's by a relative error of at most 0.0055.
Values may be sent and summed in bfloat16 or wider, within the bound.
No kernel may reach another device: no remote copies, remote signals or barrier semaphores. Data moves between devices by JAX's collectives and lax.ppermute only.
A program may use at most 128 MiB of HBM per device.

```python
import math
import jax
import jax.numpy as jnp
from jax import lax

NT = 512
NR = 256
NZ = 1024
MODES = 168


def level_of(key, dims, pieces, smallest, largest):
    def one(dim, parts):
        draws = jax.random.uniform(jax.random.fold_in(jax.random.fold_in(key, 6), dim), (parts,), jnp.float32, smallest / len(pieces), largest / len(pieces))
        return jnp.repeat(jnp.exp(draws), dims[dim] // parts).reshape((-1,) + (1,) * (len(dims) - dim - 1))

    loudness = one(*pieces[0])
    for cut in pieces[1:]:
        loudness = loudness * one(*cut)
    return loudness


def scatter_about(own_key, extent, deviation, limit, split=(), held_as=jnp.bfloat16):
    result = jax.random.normal(own_key, extent, jnp.float32) * deviation
    if len(split) > 0:
        result = level_of(own_key, extent, split, -0.22, 0.18) * result
    return jnp.clip(result, min=-limit, max=limit).astype(held_as)


def setup_inputs(seed: int = 0) -> dict:
    arg_keys = jax.random.split(jax.random.key(seed), 10)
    velocity = scatter_about(arg_keys[0], (3, NT, NZ, NR), 1.0, 6.0, ((1, 8), (2, 32)))
    adj_temp = scatter_about(arg_keys[1], (NT, NZ, NR), 1.0, 6.0, ((0, 8), (1, 32)))
    radial_div = scatter_about(arg_keys[2], (NR, NR), NR ** -0.5, 0.375)
    reciprocal_distance = jnp.clip(jnp.exp(jax.random.uniform(arg_keys[3], (NR,), jnp.float32, math.log(0.002), math.log(0.02))), 0.002, 0.02)
    radial_basis = scatter_about(arg_keys[4], (MODES, NR, NR), NR ** -0.5, 0.375, ((0, 8),))
    radial_eig = jnp.clip(jnp.exp(math.log(8.0) - 2.7725887 * jax.random.uniform(arg_keys[5], (MODES, NR), jnp.float32) ** level_of(arg_keys[5], (MODES, NR), ((0, 8),), -0.2, 0.2)), 0.5, 8.0)
    axial_diff = scatter_about(arg_keys[6], (NZ, NZ), NZ ** -0.5, 0.1875)
    axial_basis = scatter_about(arg_keys[7], (NZ, NZ), NZ ** -0.5, 0.1875)
    axial_eig = jnp.clip(jnp.exp(jax.random.uniform(arg_keys[8], (NZ,), jnp.float32, math.log(0.5), math.log(8.0))), 0.5, 8.0)
    return dict(velocity=velocity, adj_temp=adj_temp, radial_div=radial_div, reciprocal_distance=reciprocal_distance, radial_basis=radial_basis, radial_eig=radial_eig, axial_diff=axial_diff, axial_basis=axial_basis, axial_eig=axial_eig)


HEAT_OFFSET = 1.0

def azimuth_table(first_mode, mode_count, first_angle, angle_count, circle):
    mode_ids = jnp.arange(mode_count, dtype=jnp.int32) + first_mode
    angle_ids = jnp.arange(angle_count, dtype=jnp.int32) + first_angle
    phase_index = mode_ids[:, None] * angle_ids[None, :] % circle
    angle_value = phase_index.astype(jnp.float32) * (2.0 * math.pi / circle)
    norm_factor = 1.0 / math.sqrt(circle)
    wave_table = jnp.stack([jnp.cos(angle_value) * norm_factor, -jnp.sin(angle_value) * norm_factor], axis=1)
    return wave_table.astype(jnp.bfloat16).reshape(mode_count * 2, angle_count)

def reference(velocity, adj_temp, radial_div, reciprocal_distance, radial_basis, radial_eig, axial_diff, axial_basis, axial_eig):
    highest = lax.Precision.HIGHEST
    fluxes = (velocity.astype(jnp.float32) * adj_temp.astype(jnp.float32)[None]).astype(jnp.bfloat16)
    fields = jnp.concatenate([fluxes, adj_temp[None]], axis=0)
    wave_table = azimuth_table(0, MODES, 0, NT, NT).astype(jnp.float32)

    def transform(field):
        flat_field = field.reshape(NT, NZ * NR).astype(jnp.float32)
        return jnp.dot(wave_table, flat_field, precision=highest).astype(jnp.bfloat16)
    harmonic_amplitudes = lax.map(transform, fields).reshape(4, MODES, 2, NZ, NR)
    harmonic_amplitudes = jnp.moveaxis(harmonic_amplitudes, 1, 0)
    axial_matrix = axial_diff.astype(jnp.float32)
    axial_vectors = axial_basis.astype(jnp.float32)
    divergence = radial_div.astype(jnp.float32)
    mode_values = jnp.arange(MODES).astype(jnp.float32)

    def one_mode(items):
        harmonic_amplitude, radial_vectors, radial_values, harmonic_coefficient = items
        radial_flux = harmonic_amplitude[0]
        angular_flux = harmonic_amplitude[1]
        axial_flux = harmonic_amplitude[2]
        thermal_state = harmonic_amplitude[3]
        cylinder_aggregate = jnp.einsum('pzj,rj->pzr', radial_flux.astype(jnp.float32), divergence, precision=highest)
        eigenbasis_projection = jnp.stack([-angular_flux[1], angular_flux[0]], axis=0).astype(jnp.float32)
        forcing_contribution = (HEAT_OFFSET * thermal_state.astype(jnp.float32) + cylinder_aggregate + harmonic_coefficient * reciprocal_distance * eigenbasis_projection).astype(jnp.bfloat16)
        vectors = radial_vectors.astype(jnp.float32)
        source_hat = jnp.einsum('pzr,ri->piz', forcing_contribution.astype(jnp.float32), vectors, precision=highest)
        flux_hat = jnp.einsum('pzr,ri->piz', axial_flux.astype(jnp.float32), vectors, precision=highest)
        combined = source_hat + jnp.einsum('pij,zj->piz', flux_hat, axial_matrix, precision=highest)
        coefficients = jnp.einsum('piz,zk->pik', combined, axial_vectors, precision=highest)
        coefficients = coefficients / (radial_values[None, :, None] + axial_eig[None, None, :] + HEAT_OFFSET)
        returned = jnp.einsum('pik,zk->piz', coefficients, axial_vectors, precision=highest)
        return jnp.einsum('piz,ri->pzr', returned, vectors, precision=highest)
    return lax.map(one_mode, (harmonic_amplitudes, radial_basis, radial_eig, mode_values))
```

```python
import functools
import math

import jax
import jax.numpy as jnp
from jax import lax
from jax.experimental import pallas as pl
from jax.experimental.pallas import tpu as pltpu
from jax.sharding import PartitionSpec as P

HEAT_OFFSET = 1.0
BF = jnp.bfloat16
F32 = jnp.float32
NT_DIMS = (((1,), (1,)), ((), ()))
VMEM_BYTES = 48 * 1024 * 1024


def azimuth_table(mode_count, angle_count, circle):
    mode_ids = jnp.arange(mode_count, dtype=jnp.int32)
    angle_ids = jnp.arange(angle_count, dtype=jnp.int32)
    phase_index = mode_ids[:, None] * angle_ids[None, :] % circle
    angle_value = phase_index.astype(F32) * (2.0 * math.pi / circle)
    norm_factor = 1.0 / math.sqrt(circle)
    return jnp.concatenate(
        [jnp.cos(angle_value) * norm_factor, -jnp.sin(angle_value) * norm_factor], axis=0
    ).astype(BF)


def vmem():
    return pl.BlockSpec(memory_space=pltpu.VMEM)


def flux_kernel(v_ref, t_ref, d_ref, x_ref):
    t_rows, z_rows, r_rows = t_ref.shape
    temp = t_ref[...].astype(F32)

    def put(field, value):
        value = value.reshape(z_rows, t_rows, r_rows)
        for group in range(4):
            for half in range(2):
                x_ref[group * 2 + half, field] = value[
                    group * 8 : group * 8 + 8, :, half * 128 : half * 128 + 128
                ]

    def flux(c):
        product = v_ref[c].astype(F32) * temp
        return jnp.swapaxes(product, 0, 1).astype(BF)

    put(1, flux(1))
    put(2, flux(2))
    radial = flux(0).reshape(z_rows * t_rows, r_rows)
    turned_temp = jnp.swapaxes(temp, 0, 1).reshape(z_rows * t_rows, r_rows)
    div = lax.dot_general(radial, d_ref[...], NT_DIMS, preferred_element_type=F32)
    put(0, (HEAT_OFFSET * turned_temp + div).astype(BF))


def flux_call(velocity, adj_temp, radial_div):
    _, nt, nz, nr = velocity.shape
    step = 16
    return pl.pallas_call(
        flux_kernel,
        grid=(nt // step,),
        in_specs=[
            pl.BlockSpec((3, step, nz, nr), lambda i: (0, i, 0, 0)),
            pl.BlockSpec((step, nz, nr), lambda i: (i, 0, 0)),
            pl.BlockSpec((nr, nr), lambda i: (0, 0)),
        ],
        out_specs=pl.BlockSpec((8, 3, 8, step, 128), lambda i: (0, 0, 0, i, 0)),
        out_shape=jax.ShapeDtypeStruct((8, 3, 8, nt, 128), BF),
        compiler_params=pltpu.CompilerParams(vmem_limit_bytes=VMEM_BYTES),
        name="flux",
    )(velocity, adj_temp, radial_div)


def spectra_kernel(x_ref, w_ref, recip_ref, y_ref, u_ref):
    rows = w_ref.shape[0]
    modes = rows // 2
    table = w_ref[...]
    mode_id = lax.broadcasted_iota(jnp.int32, (modes, 128), 0).astype(F32)
    scale = mode_id * recip_ref[...]
    scale = jnp.concatenate([scale, scale], axis=0)
    scale = jnp.concatenate([scale, scale], axis=1)
    for z in range(0, 8, 2):

        def transform(field):
            columns = [
                jnp.concatenate([x_ref[s, field, z + k] for s in range(8)], axis=0)
                for k in range(2)
            ]
            return jnp.dot(
                table, jnp.concatenate(columns, axis=1), preferred_element_type=F32
            )

        angular = transform(1).astype(BF).astype(F32)
        turned = jnp.concatenate([-angular[modes:], angular[:modes]], axis=0)
        source = transform(0) + scale * turned
        axial = transform(2)
        for k in range(2):
            lanes = slice(k * 128, k * 128 + 128)
            u_ref[pl.ds(z + k, rows, stride=16), :] = source[:, lanes]
            u_ref[pl.ds(8 + z + k, rows, stride=16), :] = axial[:, lanes]
    block = modes // 8
    for row in range(8):
        for part in range(2):
            first = (part * modes + row * block) * 16
            mine = u_ref[first : first + 16 * 16, :].reshape(16, 16, 128)
            y_ref[row, :, part, 0:16, :] = mine.astype(BF)
            for extra in range(block - 16):
                at = first + (16 + extra) * 16
                for core in range(2):
                    y_ref[row, 2 * extra + part, core, 16:24, :] = u_ref[
                        at + 8 * core : at + 8 * core + 8, :
                    ].astype(BF)
        for chip in range(2 * (block - 16), 16):
            y_ref[row, chip, :, 16:24, :] = jnp.zeros((2, 8, 128), BF)


def spectra_call(fields, table, recip_half):
    return pl.pallas_call(
        spectra_kernel,
        in_specs=[vmem()] * 3,
        out_specs=vmem(),
        out_shape=jax.ShapeDtypeStruct((8, 16, 2, 24, 128), BF),
        scratch_shapes=[pltpu.VMEM((table.shape[0] * 16, 128), F32)],
        compiler_params=pltpu.CompilerParams(vmem_limit_bytes=VMEM_BYTES),
        name="spectra",
    )(fields, table, recip_half)


def axial_solve(hs_ref, hf_ref, low_ref, a_ref, bt_ref, b_ref, r_ref, lam_ref, mu_ref, put):
    nz = hs_ref.shape[0]
    tile = 256
    flux = hf_ref[...].astype(BF)
    for at in range(0, nz, tile):
        combined = hs_ref[at : at + tile, :] + jnp.dot(
            a_ref[at : at + tile, :], flux, preferred_element_type=F32
        )
        low_ref[at : at + tile, :] = combined.astype(BF)
    combined = low_ref[...]
    for at in range(0, nz, tile):
        coefficient = jnp.dot(bt_ref[at : at + tile, :], combined, preferred_element_type=F32)
        coefficient = coefficient / (lam_ref[...] + mu_ref[at : at + tile, :] + HEAT_OFFSET)
        hf_ref[at : at + tile, :] = coefficient
    coefficients = hf_ref[...].astype(BF)
    out_rows = b_ref.shape[0]
    for at in range(0, out_rows, tile):
        returned = jnp.dot(b_ref[at : at + tile, :], coefficients, preferred_element_type=F32)
        value = lax.dot_general(
            returned.astype(BF), r_ref[...], NT_DIMS, preferred_element_type=F32
        )
        put(at, tile, value.astype(BF))


def whole_kernel(y_ref, a_ref, bt_ref, b_ref, r_ref, lam_ref, mu_ref, o_ref, hs_ref, hf_ref, low_ref):
    hs4 = hs_ref.reshape(32, 4, 8, 256)
    hf4 = hf_ref.reshape(32, 4, 8, 256)
    for group in range(4):
        left = jnp.concatenate(
            [y_ref[2 * group + half, :, 0:16, :].reshape(512, 128) for half in range(2)], axis=1
        )
        hat = jnp.dot(left, r_ref[...], preferred_element_type=F32).reshape(32, 2, 8, 256)
        hs4[:, group] = hat[:, 0]
        hf4[:, group] = hat[:, 1]

    def put(at, tile, value):
        o_ref[at // 32 : (at + tile) // 32] = value.reshape(tile // 32, 32, 256)

    axial_solve(hs_ref, hf_ref, low_ref, a_ref, bt_ref, b_ref, r_ref, lam_ref, mu_ref, put)


def shared_kernel(
    core_ref, own_ref, other_ref, whole_ref, a_ref, bt_ref, b_ref, r_ref, lam_ref, mu_ref,
    o_ref, hs_ref, hf_ref, low_ref,
):
    first = core_ref[0] == 0
    hs4 = hs_ref.reshape(32, 4, 8, 256)
    hf4 = hf_ref.reshape(32, 4, 8, 256)
    for group in range(4):

        def hat(ref):
            left = jnp.concatenate(
                [ref[2 * group + half].astype(F32).reshape(256, 128) for half in range(2)], axis=1
            )
            return jnp.dot(
                left.astype(BF), r_ref[...], preferred_element_type=F32
            ).reshape(32, 8, 256)

        own = hat(own_ref)
        other = hat(other_ref)
        hs4[:, group] = jnp.where(first, own, other)
        hf4[:, group] = jnp.where(first, other, own)
    o_ref[:, 0:32, :] = whole_ref[...]

    def put(at, tile, value):
        o_ref[at // 16 : (at + tile) // 16, 32:48, :] = value.reshape(tile // 16, 16, 256)

    axial_solve(hs_ref, hf_ref, low_ref, a_ref, bt_ref, b_ref, r_ref, lam_ref, mu_ref, put)


def solve_scratch():
    return [
        pltpu.VMEM((1024, 256), F32),
        pltpu.VMEM((1024, 256), F32),
        pltpu.VMEM((1024, 256), BF),
    ]


def whole_call(lines, a, bt, b, r, lam, mu):
    return pl.pallas_call(
        whole_kernel,
        in_specs=[vmem()] * 7,
        out_specs=vmem(),
        out_shape=jax.ShapeDtypeStruct((32, 32, 256), BF),
        scratch_shapes=solve_scratch(),
        compiler_params=pltpu.CompilerParams(vmem_limit_bytes=VMEM_BYTES),
        cost_estimate=pl.CostEstimate(flops=4 * 10**9, bytes_accessed=8 * 10**6, transcendentals=0),
        name="whole_pair",
    )(lines, a, bt, b, r, lam, mu)


def shared_call(core, own, other, whole, a, bt, b, r, lam, mu):
    return pl.pallas_call(
        shared_kernel,
        in_specs=[pl.BlockSpec(memory_space=pltpu.SMEM)] + [vmem()] * 9,
        out_specs=vmem(),
        out_shape=jax.ShapeDtypeStruct((32, 48, 256), BF),
        scratch_shapes=solve_scratch(),
        compiler_params=pltpu.CompilerParams(vmem_limit_bytes=VMEM_BYTES),
        name="shared_pair",
    )(core, own, other, whole, a, bt, b, r, lam, mu)


def out_kernel(p_ref, o_ref):
    o_ref[0:16] = p_ref[:, :, 0:32, :].astype(F32)
    for extra in range(o_ref.shape[0] - 16):
        for part in range(2):
            for core in range(2):
                o_ref[16 + extra, part, 16 * core : 16 * core + 16, :] = p_ref[
                    2 * extra + part, core, 32:48, :
                ].astype(F32)


def out_call(pieces, mode_rows):
    return pl.pallas_call(
        out_kernel,
        in_specs=[vmem()],
        out_specs=vmem(),
        out_shape=jax.ShapeDtypeStruct((mode_rows, 2, 32, 256), F32),
        compiler_params=pltpu.CompilerParams(vmem_limit_bytes=VMEM_BYTES),
        name="result",
    )(pieces)


def body(
    velocity,
    adj_temp,
    radial_div,
    reciprocal_distance,
    radial_basis,
    radial_eig,
    axial_diff,
    axial_basis,
    axial_eig,
):
    row_total = lax.axis_size("row")
    col_total = lax.axis_size("col")
    row_place = lax.axis_index("row")
    col_place = lax.axis_index("col")
    chip = col_place // 2
    core = col_place % 2
    mode_rows = radial_basis.shape[0]
    circle = velocity.shape[1] * row_total
    exchange = functools.partial(lax.all_to_all, split_axis=0, concat_axis=0, tiled=True)

    fields = exchange(flux_call(velocity, adj_temp, radial_div), "row")

    table = azimuth_table(mode_rows * row_total, circle, circle)
    recip_half = lax.dynamic_slice_in_dim(reciprocal_distance, (row_place % 2) * 128, 128)
    spectra = spectra_call(fields, table, recip_half[None, :])
    lines = exchange(spectra.reshape(row_total * col_total, 24, 128), ("row", "col"))
    lines = lines.reshape(row_total, col_total, 24, 128)

    own = lines[:, :, 16:24, :]
    other = lax.ppermute(own, "col", [(i, i ^ 1) for i in range(col_total)])
    basis_turned = axial_basis.T
    basis_half = lax.dynamic_index_in_dim(
        axial_basis.reshape(col_total, 2, 16, axial_basis.shape[1]), core, 1, keepdims=False
    ).reshape(col_total * 16, axial_basis.shape[1])
    shared_mode = 16 + jnp.minimum(chip, 2 * (mode_rows - 16) - 1) // 2
    mu = axial_eig[:, None]

    def pick(array, index):
        return lax.dynamic_index_in_dim(array, index, 0, keepdims=False)

    whole = whole_call(
        lines, axial_diff, basis_turned, axial_basis, pick(radial_basis, chip),
        pick(radial_eig, chip)[None, :], mu,
    )
    pieces = shared_call(
        core.reshape(1), own, other, whole, axial_diff, basis_turned, basis_half,
        pick(radial_basis, shared_mode), pick(radial_eig, shared_mode)[None, :], mu,
    )
    pieces = exchange(pieces, "col")
    return out_call(pieces.reshape(16, 2, 48, 256), mode_rows)


def solution(mesh):
    in_specs = (
        P(None, "row", "col", None),
        P("row", "col", None),
        P(),
        P(),
        P("row", None, None),
        P("row", None),
        P(),
        P(),
        P(),
    )
    out_specs = P("row", None, "col", None)
    return jax.shard_map(body, mesh=mesh, in_specs=in_specs, out_specs=out_specs, check_vma=False)
```

```python
import functools
import math

import jax
import jax.numpy as jnp
from jax import lax
from jax.experimental import pallas as pl
from jax.experimental.pallas import tpu as pltpu
from jax.sharding import PartitionSpec as P

HEAT_OFFSET = 1.0
BF = jnp.bfloat16
F32 = jnp.float32
NT_DIMS = (((1,), (1,)), ((), ()))
MIB = 1024 * 1024
SPECTRA_LIMIT = 24 * MIB
SOLVE_LIMIT = 24 * MIB


def azimuth_table(mode_count, angle_count, circle):
    mode_ids = jnp.arange(mode_count, dtype=jnp.int32)
    angle_ids = jnp.arange(angle_count, dtype=jnp.int32)
    phase_index = mode_ids[:, None] * angle_ids[None, :] % circle
    angle_value = phase_index.astype(F32) * (2.0 * math.pi / circle)
    norm_factor = 1.0 / math.sqrt(circle)
    return jnp.concatenate(
        [jnp.cos(angle_value) * norm_factor, -jnp.sin(angle_value) * norm_factor], axis=0
    ).astype(BF)


def vmem():
    return pl.BlockSpec(memory_space=pltpu.VMEM)


def flux_kernel(v_ref, t_ref, d_ref, x_ref):
    t_rows, z_rows, r_rows = t_ref.shape
    temp = t_ref[...].astype(F32)

    def put(field, value):
        value = value.reshape(z_rows, t_rows, r_rows)
        for group in range(4):
            for half in range(2):
                x_ref[group * 2 + half, field, 0] = value[
                    group * 8 : group * 8 + 8, :, half * 128 : half * 128 + 128
                ]

    def flux(c):
        product = v_ref[c].astype(F32) * temp
        return jnp.swapaxes(product, 0, 1).astype(BF)

    put(1, flux(1))
    put(2, flux(2))
    radial = flux(0).reshape(z_rows * t_rows, r_rows)
    turned_temp = jnp.swapaxes(temp, 0, 1).reshape(z_rows * t_rows, r_rows)
    div = lax.dot_general(radial, d_ref[...], NT_DIMS, preferred_element_type=F32)
    put(0, (HEAT_OFFSET * turned_temp + div).astype(BF))


def flux_call(velocity, adj_temp, radial_div):
    _, nt, nz, nr = velocity.shape
    step = 32
    return pl.pallas_call(
        flux_kernel,
        grid=(nt // step,),
        in_specs=[
            pl.BlockSpec((3, step, nz, nr), lambda i: (0, i, 0, 0)),
            pl.BlockSpec((step, nz, nr), lambda i: (i, 0, 0)),
            pl.BlockSpec((nr, nr), lambda i: (0, 0)),
        ],
        out_specs=pl.BlockSpec((8, 3, 1, 8, step, 128), lambda i: (0, 0, i, 0, 0, 0)),
        out_shape=jax.ShapeDtypeStruct((8, 3, nt // step, 8, step, 128), BF),
        compiler_params=pltpu.CompilerParams(vmem_limit_bytes=60 * MIB),
        name="flux",
    )(velocity, adj_temp, radial_div)


def spectra_kernel(x_ref, w_ref, recip_ref, *rest):
    y_ref, u_ref = rest[-2:]
    rows = w_ref.shape[0]
    modes = rows // 2
    table = w_ref[...]
    mode_id = lax.broadcasted_iota(jnp.int32, (modes, 128), 0).astype(F32)
    scale = mode_id * recip_ref[...]
    scale = jnp.concatenate([scale, scale], axis=0)
    scale = jnp.concatenate([scale, scale], axis=1)
    z = 2 * pl.program_id(0)

    def transform(field):
        columns = [
            jnp.concatenate(
                [x_ref[s, field, h, k] for s in range(8) for h in range(2)], axis=0
            )
            for k in range(2)
        ]
        return jnp.dot(table, jnp.concatenate(columns, axis=1), preferred_element_type=F32)

    angular = transform(1).astype(BF).astype(F32)
    turned = jnp.concatenate([-angular[modes:], angular[:modes]], axis=0)
    source = transform(0) + scale * turned
    axial = transform(2)
    for k in range(2):
        lanes = slice(k * 128, k * 128 + 128)
        u_ref[pl.ds(z + k, rows, stride=16), :] = source[:, lanes]
        u_ref[pl.ds(8 + z + k, rows, stride=16), :] = axial[:, lanes]

    @pl.when(pl.program_id(0) == pl.num_programs(0) - 1)
    def _():
        write_messages(u_ref, y_ref, modes)


def write_messages(u_ref, y_ref, modes):
    block = modes // 8
    for row in range(8):
        for part in range(2):
            first = (part * modes + row * block) * 16
            mine = u_ref[first : first + 16 * 16, :].reshape(16, 16, 128)
            y_ref[row, :, part, 0:16, :] = mine.astype(BF)
            for extra in range(block - 16):
                at = first + (16 + extra) * 16
                for core in range(2):
                    y_ref[row, 2 * extra + part, core, 16:24, :] = u_ref[
                        at + 8 * core : at + 8 * core + 8, :
                    ].astype(BF)
        for chip in range(2 * (block - 16), 16):
            y_ref[row, chip, :, 16:24, :] = jnp.zeros((2, 8, 128), BF)


def spectra_call(fields, table, recip_half, later):
    return pl.pallas_call(
        spectra_kernel,
        grid=(4,),
        in_specs=[pl.BlockSpec((8, 3, 2, 2, 32, 128), lambda i: (0, 0, 0, i, 0, 0))]
        + [vmem()] * 2
        + [pl.BlockSpec(memory_space=pl.ANY)] * len(later),
        out_specs=vmem(),
        out_shape=jax.ShapeDtypeStruct((8, 16, 2, 24, 128), BF),
        scratch_shapes=[pltpu.VMEM((table.shape[0] * 16, 128), F32)],
        compiler_params=pltpu.CompilerParams(vmem_limit_bytes=SPECTRA_LIMIT),
        name="spectra",
    )(fields, table, recip_half, *later)


def axial_solve(hs_ref, hf_ref, low_ref, a_ref, bt_ref, b_ref, r_ref, lam_ref, mu_ref, put):
    nz = hs_ref.shape[0]
    tile = 256
    flux = hf_ref[...].astype(BF)
    shift = jnp.transpose(jnp.broadcast_to(mu_ref[...], (8, nz)))[:, 0:1] + HEAT_OFFSET
    for at in range(0, nz, tile):
        combined = hs_ref[at : at + tile, :] + jnp.dot(
            a_ref[at : at + tile, :], flux, preferred_element_type=F32
        )
        low_ref[at : at + tile, :] = combined.astype(BF)
    combined = low_ref[...]
    for at in range(0, nz, tile):
        coefficient = jnp.dot(bt_ref[at : at + tile, :], combined, preferred_element_type=F32)
        coefficient = coefficient / (lam_ref[...] + shift[at : at + tile, :])
        hf_ref[at : at + tile, :] = coefficient
    coefficients = hf_ref[...].astype(BF)
    out_rows = b_ref.shape[0]
    for at in range(0, out_rows, tile):
        returned = jnp.dot(b_ref[at : at + tile, :], coefficients, preferred_element_type=F32)
        value = lax.dot_general(
            returned.astype(BF), r_ref[...], NT_DIMS, preferred_element_type=F32
        )
        put(at, tile, value.astype(BF))


def whole_kernel(y_ref, a_ref, bt_ref, b_ref, r_ref, lam_ref, mu_ref, o_ref, hs_ref, hf_ref, low_ref):
    hs4 = hs_ref.reshape(32, 4, 8, 256)
    hf4 = hf_ref.reshape(32, 4, 8, 256)
    for group in range(4):
        left = jnp.concatenate(
            [y_ref[2 * group + half, :, 0:16, :].reshape(512, 128) for half in range(2)], axis=1
        )
        hat = jnp.dot(left, r_ref[...], preferred_element_type=F32).reshape(32, 2, 8, 256)
        hs4[:, group] = hat[:, 0]
        hf4[:, group] = hat[:, 1]

    def put(at, tile, value):
        o_ref[at // 32 : (at + tile) // 32] = value.reshape(tile // 32, 32, 256)

    axial_solve(hs_ref, hf_ref, low_ref, a_ref, bt_ref, b_ref, r_ref, lam_ref, mu_ref, put)


def shared_kernel(
    core_ref, own_ref, other_ref, whole_ref, a_ref, bt_ref, b_ref, r_ref, lam_ref, mu_ref,
    o_ref, hs_ref, hf_ref, low_ref,
):
    first = core_ref[0] == 0
    hs4 = hs_ref.reshape(32, 4, 8, 256)
    hf4 = hf_ref.reshape(32, 4, 8, 256)
    for group in range(4):

        def hat(ref):
            left = jnp.concatenate(
                [ref[2 * group + half].astype(F32).reshape(256, 128) for half in range(2)], axis=1
            )
            return jnp.dot(
                left.astype(BF), r_ref[...], preferred_element_type=F32
            ).reshape(32, 8, 256)

        own = hat(own_ref)
        other = hat(other_ref)
        hs4[:, group] = jnp.where(first, own, other)
        hf4[:, group] = jnp.where(first, other, own)
    o_ref[:, 0:32, :] = whole_ref[...]

    def put(at, tile, value):
        o_ref[at // 16 : (at + tile) // 16, 32:48, :] = value.reshape(tile // 16, 16, 256)

    axial_solve(hs_ref, hf_ref, low_ref, a_ref, bt_ref, b_ref, r_ref, lam_ref, mu_ref, put)


def solve_scratch():
    return [
        pltpu.VMEM((1024, 256), F32),
        pltpu.VMEM((1024, 256), F32),
        pltpu.VMEM((1024, 256), BF),
    ]


def whole_call(lines, a, bt, b, r, lam, mu):
    return pl.pallas_call(
        whole_kernel,
        in_specs=[vmem()] * 7,
        out_specs=vmem(),
        out_shape=jax.ShapeDtypeStruct((32, 32, 256), BF),
        scratch_shapes=solve_scratch(),
        compiler_params=pltpu.CompilerParams(vmem_limit_bytes=SOLVE_LIMIT),
        cost_estimate=pl.CostEstimate(flops=4 * 10**9, bytes_accessed=8 * 10**6, transcendentals=0),
        name="whole_pair",
    )(lines, a, bt, b, r, lam, mu)


def shared_call(core, own, other, whole, a, bt, b, r, lam, mu):
    return pl.pallas_call(
        shared_kernel,
        in_specs=[pl.BlockSpec(memory_space=pltpu.SMEM)] + [vmem()] * 9,
        out_specs=vmem(),
        out_shape=jax.ShapeDtypeStruct((32, 48, 256), BF),
        scratch_shapes=solve_scratch(),
        compiler_params=pltpu.CompilerParams(vmem_limit_bytes=SOLVE_LIMIT),
        name="shared_pair",
    )(core, own, other, whole, a, bt, b, r, lam, mu)


def out_kernel(p_ref, o_ref):
    o_ref[0:16] = p_ref[:, :, 0:32, :].astype(F32)
    for extra in range(o_ref.shape[0] - 16):
        for part in range(2):
            for core in range(2):
                o_ref[16 + extra, part, 16 * core : 16 * core + 16, :] = p_ref[
                    2 * extra + part, core, 32:48, :
                ].astype(F32)


def out_call(pieces, mode_rows):
    return pl.pallas_call(
        out_kernel,
        in_specs=[vmem()],
        out_specs=vmem(),
        out_shape=jax.ShapeDtypeStruct((mode_rows, 2, 32, 256), F32),
        compiler_params=pltpu.CompilerParams(vmem_limit_bytes=SOLVE_LIMIT),
        name="result",
    )(pieces)


def body(
    velocity,
    adj_temp,
    radial_div,
    reciprocal_distance,
    radial_basis,
    radial_eig,
    axial_diff,
    axial_basis,
    axial_eig,
):
    row_total = lax.axis_size("row")
    col_total = lax.axis_size("col")
    row_place = lax.axis_index("row")
    col_place = lax.axis_index("col")
    chip = col_place // 2
    core = col_place % 2
    mode_rows = radial_basis.shape[0]
    circle = velocity.shape[1] * row_total
    exchange = functools.partial(lax.all_to_all, split_axis=0, concat_axis=0, tiled=True)

    fields = exchange(flux_call(velocity, adj_temp, radial_div), "row")

    def pick(array, index):
        return lax.dynamic_index_in_dim(array, index, 0, keepdims=False)

    table = azimuth_table(mode_rows * row_total, circle, circle)
    recip_half = lax.dynamic_slice_in_dim(reciprocal_distance, (row_place % 2) * 128, 128)
    basis_turned = axial_basis.T
    basis_half = pick(
        axial_basis.reshape(col_total, 2, 16, axial_basis.shape[1]).swapaxes(0, 1), core
    ).reshape(col_total * 16, axial_basis.shape[1])
    shared_mode = 16 + jnp.minimum(chip, 2 * (mode_rows - 16) - 1) // 2
    mu = axial_eig[None, :]
    whole_basis, shared_basis = pick(radial_basis, chip), pick(radial_basis, shared_mode)
    whole_eig, shared_eig = pick(radial_eig, chip)[None, :], pick(radial_eig, shared_mode)[None, :]

    later = [whole_basis, shared_basis, whole_eig, shared_eig]
    fields, later = lax.optimization_barrier((fields, later))
    whole_basis, shared_basis, whole_eig, shared_eig = later
    spectra = spectra_call(fields, table, recip_half[None, :], [basis_turned, basis_half])
    lines = exchange(spectra.reshape(row_total * col_total, 24, 128), ("row", "col"))
    lines = lines.reshape(row_total, col_total, 24, 128)

    own = lines[:, :, 16:24, :]
    other = lax.ppermute(own, "col", [(i, i ^ 1) for i in range(col_total)])
    whole = whole_call(
        lines, axial_diff, basis_turned, axial_basis, whole_basis, whole_eig, mu
    )
    pieces = shared_call(
        core.reshape(1), own, other, whole, axial_diff, basis_turned, basis_half,
        shared_basis, shared_eig, mu,
    )
    pieces = exchange(pieces, "col")
    return out_call(pieces.reshape(16, 2, 48, 256), mode_rows)


def solution(mesh):
    in_specs = (
        P(None, "row", "col", None),
        P("row", "col", None),
        P(),
        P(),
        P("row", None, None),
        P("row", None),
        P(),
        P(),
        P(),
    )
    out_specs = P("row", None, "col", None)
    return jax.shard_map(body, mesh=mesh, in_specs=in_specs, out_specs=out_specs, check_vma=False)
```

```python
import functools
import math

import jax
import jax.numpy as jnp
from jax import lax
from jax.experimental import pallas as pl
from jax.experimental.pallas import tpu as pltpu
from jax.sharding import PartitionSpec as P

HEAT_OFFSET = 1.0
BF = jnp.bfloat16
F32 = jnp.float32
NT_DIMS = (((1,), (1,)), ((), ()))
MIB = 1024 * 1024
SPECTRA_LIMIT = 24 * MIB
SOLVE_LIMIT = 24 * MIB


def azimuth_table(mode_count, angle_count, circle):
    mode_ids = jnp.arange(mode_count, dtype=jnp.int32)
    angle_ids = jnp.arange(angle_count, dtype=jnp.int32)
    phase_index = mode_ids[:, None] * angle_ids[None, :] % circle
    angle_value = phase_index.astype(F32) * (2.0 * math.pi / circle)
    norm_factor = 1.0 / math.sqrt(circle)
    return jnp.concatenate(
        [jnp.cos(angle_value) * norm_factor, -jnp.sin(angle_value) * norm_factor], axis=0
    ).astype(BF)


def vmem():
    return pl.BlockSpec(memory_space=pltpu.VMEM)


def flux_kernel(v_ref, t_ref, d_ref, x_ref):
    t_rows, z_rows, r_rows = t_ref.shape
    temp = t_ref[...].astype(F32)

    def put(field, value):
        value = value.reshape(z_rows, t_rows, r_rows)
        for group in range(4):
            for half in range(2):
                x_ref[group * 2 + half, field, 0] = value[
                    group * 8 : group * 8 + 8, :, half * 128 : half * 128 + 128
                ]

    def flux(c):
        product = v_ref[c].astype(F32) * temp
        return jnp.swapaxes(product, 0, 1).astype(BF)

    put(1, flux(1))
    put(2, flux(2))
    radial = flux(0).reshape(z_rows * t_rows, r_rows)
    turned_temp = jnp.swapaxes(temp, 0, 1).reshape(z_rows * t_rows, r_rows)
    div = lax.dot_general(radial, d_ref[...], NT_DIMS, preferred_element_type=F32)
    put(0, (HEAT_OFFSET * turned_temp + div).astype(BF))


def flux_call(velocity, adj_temp, radial_div):
    _, nt, nz, nr = velocity.shape
    step = 32
    return pl.pallas_call(
        flux_kernel,
        grid=(nt // step,),
        in_specs=[
            pl.BlockSpec((3, step, nz, nr), lambda i: (0, i, 0, 0)),
            pl.BlockSpec((step, nz, nr), lambda i: (i, 0, 0)),
            pl.BlockSpec((nr, nr), lambda i: (0, 0)),
        ],
        out_specs=pl.BlockSpec((8, 3, 1, 8, step, 128), lambda i: (0, 0, i, 0, 0, 0)),
        out_shape=jax.ShapeDtypeStruct((8, 3, nt // step, 8, step, 128), BF),
        compiler_params=pltpu.CompilerParams(vmem_limit_bytes=60 * MIB),
        name="flux",
    )(velocity, adj_temp, radial_div)


def spectra_kernel(x_ref, w_ref, recip_ref, y_ref, u_ref):
    rows = w_ref.shape[0]
    modes = rows // 2
    table = w_ref[...]
    mode_id = lax.broadcasted_iota(jnp.int32, (modes, 128), 0).astype(F32)
    scale = mode_id * recip_ref[...]
    scale = jnp.concatenate([scale, scale], axis=0)
    scale = jnp.concatenate([scale, scale], axis=1)
    for z in range(0, 8, 2):

        def transform(field):
            columns = [
                jnp.concatenate(
                    [x_ref[s, field, h, z + k] for s in range(8) for h in range(2)], axis=0
                )
                for k in range(2)
            ]
            return jnp.dot(
                table, jnp.concatenate(columns, axis=1), preferred_element_type=F32
            )

        angular = transform(1).astype(BF).astype(F32)
        turned = jnp.concatenate([-angular[modes:], angular[:modes]], axis=0)
        source = transform(0) + scale * turned
        axial = transform(2)
        for k in range(2):
            lanes = slice(k * 128, k * 128 + 128)
            u_ref[pl.ds(z + k, rows, stride=16), :] = source[:, lanes]
            u_ref[pl.ds(8 + z + k, rows, stride=16), :] = axial[:, lanes]
    block = modes // 8
    for row in range(8):
        for part in range(2):
            first = (part * modes + row * block) * 16
            mine = u_ref[first : first + 16 * 16, :].reshape(16, 16, 128)
            y_ref[row, :, part, 0:16, :] = mine.astype(BF)
            for extra in range(block - 16):
                at = first + (16 + extra) * 16
                for core in range(2):
                    y_ref[row, 2 * extra + part, core, 16:24, :] = u_ref[
                        at + 8 * core : at + 8 * core + 8, :
                    ].astype(BF)
        for chip in range(2 * (block - 16), 16):
            y_ref[row, chip, :, 16:24, :] = jnp.zeros((2, 8, 128), BF)


def spectra_call(fields, table, recip_half):
    return pl.pallas_call(
        spectra_kernel,
        in_specs=[vmem()] * 3,
        out_specs=vmem(),
        out_shape=jax.ShapeDtypeStruct((8, 16, 2, 24, 128), BF),
        scratch_shapes=[pltpu.VMEM((table.shape[0] * 16, 128), F32)],
        compiler_params=pltpu.CompilerParams(vmem_limit_bytes=SPECTRA_LIMIT),
        name="spectra",
    )(fields, table, recip_half)


def axial_solve(hs_ref, hf_ref, low_ref, a_ref, bt_ref, b_ref, r_ref, lam_ref, mu_ref, put):
    nz = hs_ref.shape[0]
    tile = 256
    flux = hf_ref[...].astype(BF)
    shift = jnp.transpose(jnp.broadcast_to(mu_ref[...], (8, nz)))[:, 0:1] + HEAT_OFFSET
    for at in range(0, nz, tile):
        combined = hs_ref[at : at + tile, :] + jnp.dot(
            a_ref[at : at + tile, :], flux, preferred_element_type=F32
        )
        low_ref[at : at + tile, :] = combined.astype(BF)
    combined = low_ref[...]
    for at in range(0, nz, tile):
        coefficient = jnp.dot(bt_ref[at : at + tile, :], combined, preferred_element_type=F32)
        coefficient = coefficient / (lam_ref[...] + shift[at : at + tile, :])
        hf_ref[at : at + tile, :] = coefficient
    coefficients = hf_ref[...].astype(BF)
    out_rows = b_ref.shape[0]
    for at in range(0, out_rows, tile):
        returned = jnp.dot(b_ref[at : at + tile, :], coefficients, preferred_element_type=F32)
        value = lax.dot_general(
            returned.astype(BF), r_ref[...], NT_DIMS, preferred_element_type=F32
        )
        put(at, tile, value.astype(BF))


def whole_kernel(y_ref, a_ref, bt_ref, b_ref, r_ref, lam_ref, mu_ref, o_ref, hs_ref, hf_ref, low_ref):
    hs4 = hs_ref.reshape(32, 4, 8, 256)
    hf4 = hf_ref.reshape(32, 4, 8, 256)
    for group in range(4):
        left = jnp.concatenate(
            [y_ref[2 * group + half, :, 0:16, :].reshape(512, 128) for half in range(2)], axis=1
        )
        hat = jnp.dot(left, r_ref[...], preferred_element_type=F32).reshape(32, 2, 8, 256)
        hs4[:, group] = hat[:, 0]
        hf4[:, group] = hat[:, 1]

    def put(at, tile, value):
        o_ref[at // 32 : (at + tile) // 32] = value.reshape(tile // 32, 32, 256)

    axial_solve(hs_ref, hf_ref, low_ref, a_ref, bt_ref, b_ref, r_ref, lam_ref, mu_ref, put)


def shared_kernel(
    core_ref, own_ref, other_ref, whole_ref, a_ref, bt_ref, b_ref, r_ref, lam_ref, mu_ref,
    o_ref, hs_ref, hf_ref, low_ref,
):
    first = core_ref[0] == 0
    hs4 = hs_ref.reshape(32, 4, 8, 256)
    hf4 = hf_ref.reshape(32, 4, 8, 256)
    for group in range(4):

        def hat(ref):
            left = jnp.concatenate(
                [ref[2 * group + half].astype(F32).reshape(256, 128) for half in range(2)], axis=1
            )
            return jnp.dot(
                left.astype(BF), r_ref[...], preferred_element_type=F32
            ).reshape(32, 8, 256)

        own = hat(own_ref)
        other = hat(other_ref)
        hs4[:, group] = jnp.where(first, own, other)
        hf4[:, group] = jnp.where(first, other, own)
    o_ref[:, 0:32, :] = whole_ref[...]

    def put(at, tile, value):
        o_ref[at // 16 : (at + tile) // 16, 32:48, :] = value.reshape(tile // 16, 16, 256)

    axial_solve(hs_ref, hf_ref, low_ref, a_ref, bt_ref, b_ref, r_ref, lam_ref, mu_ref, put)


def solve_scratch():
    return [
        pltpu.VMEM((1024, 256), F32),
        pltpu.VMEM((1024, 256), F32),
        pltpu.VMEM((1024, 256), BF),
    ]


def whole_call(lines, a, bt, b, r, lam, mu):
    return pl.pallas_call(
        whole_kernel,
        in_specs=[vmem()] * 7,
        out_specs=vmem(),
        out_shape=jax.ShapeDtypeStruct((32, 32, 256), BF),
        scratch_shapes=solve_scratch(),
        compiler_params=pltpu.CompilerParams(vmem_limit_bytes=SOLVE_LIMIT),
        cost_estimate=pl.CostEstimate(flops=4 * 10**9, bytes_accessed=8 * 10**6, transcendentals=0),
        name="whole_pair",
    )(lines, a, bt, b, r, lam, mu)


def shared_call(core, own, other, whole, a, bt, b, r, lam, mu):
    return pl.pallas_call(
        shared_kernel,
        in_specs=[pl.BlockSpec(memory_space=pltpu.SMEM)] + [vmem()] * 9,
        out_specs=vmem(),
        out_shape=jax.ShapeDtypeStruct((32, 48, 256), BF),
        scratch_shapes=solve_scratch(),
        compiler_params=pltpu.CompilerParams(vmem_limit_bytes=SOLVE_LIMIT),
        name="shared_pair",
    )(core, own, other, whole, a, bt, b, r, lam, mu)


def out_kernel(p_ref, o_ref):
    o_ref[0:16] = p_ref[:, :, 0:32, :].astype(F32)
    for extra in range(o_ref.shape[0] - 16):
        for part in range(2):
            for core in range(2):
                o_ref[16 + extra, part, 16 * core : 16 * core + 16, :] = p_ref[
                    2 * extra + part, core, 32:48, :
                ].astype(F32)


def out_call(pieces, mode_rows):
    return pl.pallas_call(
        out_kernel,
        in_specs=[vmem()],
        out_specs=vmem(),
        out_shape=jax.ShapeDtypeStruct((mode_rows, 2, 32, 256), F32),
        compiler_params=pltpu.CompilerParams(vmem_limit_bytes=SOLVE_LIMIT),
        name="result",
    )(pieces)


def body(
    velocity,
    adj_temp,
    radial_div,
    reciprocal_distance,
    radial_basis,
    radial_eig,
    axial_diff,
    axial_basis,
    axial_eig,
):
    row_total = lax.axis_size("row")
    col_total = lax.axis_size("col")
    row_place = lax.axis_index("row")
    col_place = lax.axis_index("col")
    chip = col_place // 2
    core = col_place % 2
    mode_rows = radial_basis.shape[0]
    circle = velocity.shape[1] * row_total
    exchange = functools.partial(lax.all_to_all, split_axis=0, concat_axis=0, tiled=True)

    fields = exchange(flux_call(velocity, adj_temp, radial_div), "row")

    def pick(array, index):
        return lax.dynamic_index_in_dim(array, index, 0, keepdims=False)

    table = azimuth_table(mode_rows * row_total, circle, circle)
    recip_half = lax.dynamic_slice_in_dim(reciprocal_distance, (row_place % 2) * 128, 128)
    basis_turned = axial_basis.T
    basis_half = pick(
        axial_basis.reshape(col_total, 2, 16, axial_basis.shape[1]).swapaxes(0, 1), core
    ).reshape(col_total * 16, axial_basis.shape[1])
    shared_mode = 16 + jnp.minimum(chip, 2 * (mode_rows - 16) - 1) // 2
    mu = axial_eig[None, :]
    whole_basis, shared_basis = pick(radial_basis, chip), pick(radial_basis, shared_mode)
    whole_eig, shared_eig = pick(radial_eig, chip)[None, :], pick(radial_eig, shared_mode)[None, :]

    later = [basis_turned, basis_half, whole_basis, shared_basis, whole_eig, shared_eig]
    fields, later = lax.optimization_barrier((fields, later))
    basis_turned, basis_half, whole_basis, shared_basis, whole_eig, shared_eig = later
    spectra = spectra_call(fields, table, recip_half[None, :])
    lines = exchange(spectra.reshape(row_total * col_total, 24, 128), ("row", "col"))
    lines = lines.reshape(row_total, col_total, 24, 128)

    own = lines[:, :, 16:24, :]
    other = lax.ppermute(own, "col", [(i, i ^ 1) for i in range(col_total)])
    whole = whole_call(
        lines, axial_diff, basis_turned, axial_basis, whole_basis, whole_eig, mu
    )
    pieces = shared_call(
        core.reshape(1), own, other, whole, axial_diff, basis_turned, basis_half,
        shared_basis, shared_eig, mu,
    )
    pieces = exchange(pieces, "col")
    return out_call(pieces.reshape(16, 2, 48, 256), mode_rows)


def solution(mesh):
    in_specs = (
        P(None, "row", "col", None),
        P("row", "col", None),
        P(),
        P(),
        P("row", None, None),
        P("row", None),
        P(),
        P(),
        P(),
    )
    out_specs = P("row", None, "col", None)
    return jax.shard_map(body, mesh=mesh, in_specs=in_specs, out_specs=out_specs, check_vma=False)
```

```python
import functools
import math

import jax
import jax.numpy as jnp
from jax import lax
from jax.experimental import pallas as pl
from jax.experimental.pallas import tpu as pltpu
from jax.sharding import PartitionSpec as P

HEAT_OFFSET = 1.0
BF = jnp.bfloat16
F32 = jnp.float32
NT_DIMS = (((1,), (1,)), ((), ()))
MIB = 1024 * 1024
SPECTRA_LIMIT = 24 * MIB
SOLVE_LIMIT = 24 * MIB


def azimuth_table(mode_count, angle_count, circle):
    mode_ids = jnp.arange(mode_count, dtype=jnp.int32)
    angle_ids = jnp.arange(angle_count, dtype=jnp.int32)
    phase_index = mode_ids[:, None] * angle_ids[None, :] % circle
    angle_value = phase_index.astype(F32) * (2.0 * math.pi / circle)
    norm_factor = 1.0 / math.sqrt(circle)
    return jnp.concatenate(
        [jnp.cos(angle_value) * norm_factor, -jnp.sin(angle_value) * norm_factor], axis=0
    ).astype(BF)


def vmem():
    return pl.BlockSpec(memory_space=pltpu.VMEM)


def flux_kernel(v_ref, t_ref, d_ref, x_ref):
    t_rows, z_rows, r_rows = t_ref.shape
    temp = t_ref[...].astype(F32)

    def put(field, value):
        value = jnp.swapaxes(value, 0, 1).astype(BF)
        for group in range(4):
            for half in range(2):
                x_ref[group * 2 + half, field, 0] = value[
                    group * 8 : group * 8 + 8, :, half * 128 : half * 128 + 128
                ]

    put(1, v_ref[1].astype(F32) * temp)
    put(2, v_ref[2].astype(F32) * temp)
    radial = (v_ref[0].astype(F32) * temp).astype(BF).reshape(t_rows * z_rows, r_rows)
    div = lax.dot_general(radial, d_ref[...], NT_DIMS, preferred_element_type=F32)
    put(0, HEAT_OFFSET * temp + div.reshape(t_rows, z_rows, r_rows))


def flux_call(velocity, adj_temp, radial_div):
    _, nt, nz, nr = velocity.shape
    step = 32
    return pl.pallas_call(
        flux_kernel,
        grid=(nt // step,),
        in_specs=[
            pl.BlockSpec((3, step, nz, nr), lambda i: (0, i, 0, 0)),
            pl.BlockSpec((step, nz, nr), lambda i: (i, 0, 0)),
            pl.BlockSpec((nr, nr), lambda i: (0, 0)),
        ],
        out_specs=pl.BlockSpec((8, 3, 1, 8, step, 128), lambda i: (0, 0, i, 0, 0, 0)),
        out_shape=jax.ShapeDtypeStruct((8, 3, nt // step, 8, step, 128), BF),
        compiler_params=pltpu.CompilerParams(vmem_limit_bytes=60 * MIB),
        name="flux",
    )(velocity, adj_temp, radial_div)


def spectra_kernel(x_ref, w_ref, recip_ref, y_ref, u_ref):
    rows = w_ref.shape[0]
    modes = rows // 2
    table = w_ref[...]
    mode_id = lax.broadcasted_iota(jnp.int32, (modes, 128), 0).astype(F32)
    scale = mode_id * recip_ref[...]
    scale = jnp.concatenate([scale, scale], axis=0)
    scale = jnp.concatenate([scale, scale], axis=1)
    for z in range(0, 8, 2):

        def transform(field):
            columns = [
                jnp.concatenate(
                    [x_ref[s, field, h, z + k] for s in range(8) for h in range(2)], axis=0
                )
                for k in range(2)
            ]
            return jnp.dot(
                table, jnp.concatenate(columns, axis=1), preferred_element_type=F32
            )

        angular = transform(1).astype(BF).astype(F32)
        turned = jnp.concatenate([-angular[modes:], angular[:modes]], axis=0)
        source = transform(0) + scale * turned
        axial = transform(2)
        for k in range(2):
            lanes = slice(k * 128, k * 128 + 128)
            u_ref[pl.ds(z + k, rows, stride=16), :] = source[:, lanes]
            u_ref[pl.ds(8 + z + k, rows, stride=16), :] = axial[:, lanes]
    block = modes // 8
    for row in range(8):
        for part in range(2):
            first = (part * modes + row * block) * 16
            mine = u_ref[first : first + 16 * 16, :].reshape(16, 16, 128)
            y_ref[row, :, part, 0:16, :] = mine.astype(BF)
            for extra in range(block - 16):
                at = first + (16 + extra) * 16
                for core in range(2):
                    y_ref[row, 2 * extra + part, core, 16:24, :] = u_ref[
                        at + 8 * core : at + 8 * core + 8, :
                    ].astype(BF)
        for chip in range(2 * (block - 16), 16):
            y_ref[row, chip, :, 16:24, :] = jnp.zeros((2, 8, 128), BF)


def spectra_call(fields, table, recip_half):
    return pl.pallas_call(
        spectra_kernel,
        in_specs=[vmem()] * 3,
        out_specs=vmem(),
        out_shape=jax.ShapeDtypeStruct((8, 16, 2, 24, 128), BF),
        scratch_shapes=[pltpu.VMEM((table.shape[0] * 16 + 16, 128), F32)],
        compiler_params=pltpu.CompilerParams(vmem_limit_bytes=SPECTRA_LIMIT),
        name="spectra",
    )(fields, table, recip_half)


def axial_solve(hs_ref, hf_ref, low_ref, a_ref, bt_ref, b_ref, r_ref, lam_ref, mu_ref, put):
    nz = hs_ref.shape[0]
    tile = 512
    flux = hf_ref[...].astype(BF)
    shift = jnp.transpose(jnp.broadcast_to(mu_ref[...], (8, nz)))[:, 0:1] + HEAT_OFFSET
    for at in range(0, nz, tile):
        combined = hs_ref[at : at + tile, :] + jnp.dot(
            a_ref[at : at + tile, :], flux, preferred_element_type=F32
        )
        low_ref[at : at + tile, :] = combined.astype(BF)
    combined = low_ref[...]
    coefficients = []
    for at in range(0, nz, tile):
        coefficient = jnp.dot(bt_ref[at : at + tile, :], combined, preferred_element_type=F32)
        coefficient = coefficient / (lam_ref[...] + shift[at : at + tile, :])
        coefficients.append(coefficient.astype(BF))
    coefficients = jnp.concatenate(coefficients, axis=0)
    out_rows = b_ref.shape[0]
    for at in range(0, out_rows, tile):
        returned = jnp.dot(b_ref[at : at + tile, :], coefficients, preferred_element_type=F32)
        value = lax.dot_general(
            returned.astype(BF), r_ref[...], NT_DIMS, preferred_element_type=F32
        )
        put(at, tile, value.astype(BF))


def whole_kernel(y_ref, a_ref, bt_ref, b_ref, r_ref, lam_ref, mu_ref, o_ref, hs_ref, hf_ref, low_ref):
    hs4 = hs_ref.reshape(32, 4, 8, 256)
    hf4 = hf_ref.reshape(32, 4, 8, 256)
    for group in range(4):
        left = jnp.concatenate(
            [y_ref[2 * group + half, :, 0:16, :].reshape(512, 128) for half in range(2)], axis=1
        )
        hat = jnp.dot(left, r_ref[...], preferred_element_type=F32).reshape(32, 2, 8, 256)
        hs4[:, group] = hat[:, 0]
        hf4[:, group] = hat[:, 1]

    def put(at, tile, value):
        o_ref[at // 32 : (at + tile) // 32] = value.reshape(tile // 32, 32, 256)

    axial_solve(hs_ref, hf_ref, low_ref, a_ref, bt_ref, b_ref, r_ref, lam_ref, mu_ref, put)


def shared_kernel(
    core_ref, own_ref, other_ref, whole_ref, a_ref, bt_ref, b_ref, r_ref, lam_ref, mu_ref,
    o_ref, hs_ref, hf_ref, low_ref,
):
    first = core_ref[0] == 0
    hs4 = hs_ref.reshape(32, 4, 8, 256)
    hf4 = hf_ref.reshape(32, 4, 8, 256)
    for group in range(4):

        def hat(ref):
            left = jnp.concatenate(
                [ref[2 * group + half].astype(F32).reshape(256, 128) for half in range(2)], axis=1
            )
            return jnp.dot(
                left.astype(BF), r_ref[...], preferred_element_type=F32
            ).reshape(32, 8, 256)

        own = hat(own_ref)
        other = hat(other_ref)
        hs4[:, group] = jnp.where(first, own, other)
        hf4[:, group] = jnp.where(first, other, own)
    o_ref[:, 0:32, :] = whole_ref[...]

    def put(at, tile, value):
        o_ref[at // 16 : (at + tile) // 16, 32:48, :] = value.reshape(tile // 16, 16, 256)

    axial_solve(hs_ref, hf_ref, low_ref, a_ref, bt_ref, b_ref, r_ref, lam_ref, mu_ref, put)


def solve_scratch():
    return [
        pltpu.VMEM((1024, 256), F32),
        pltpu.VMEM((1024, 256), F32),
        pltpu.VMEM((1024, 256), BF),
    ]


def whole_call(lines, a, bt, b, r, lam, mu):
    return pl.pallas_call(
        whole_kernel,
        in_specs=[vmem()] * 7,
        out_specs=vmem(),
        out_shape=jax.ShapeDtypeStruct((32, 32, 256), BF),
        scratch_shapes=solve_scratch(),
        compiler_params=pltpu.CompilerParams(vmem_limit_bytes=SOLVE_LIMIT),
        cost_estimate=pl.CostEstimate(flops=4 * 10**9, bytes_accessed=8 * 10**6, transcendentals=0),
        name="whole_pair",
    )(lines, a, bt, b, r, lam, mu)


def shared_call(core, own, other, whole, a, bt, b, r, lam, mu):
    return pl.pallas_call(
        shared_kernel,
        in_specs=[pl.BlockSpec(memory_space=pltpu.SMEM)] + [vmem()] * 9,
        out_specs=vmem(),
        out_shape=jax.ShapeDtypeStruct((32, 48, 256), BF),
        scratch_shapes=solve_scratch(),
        compiler_params=pltpu.CompilerParams(vmem_limit_bytes=SOLVE_LIMIT),
        name="shared_pair",
    )(core, own, other, whole, a, bt, b, r, lam, mu)


def out_kernel(p_ref, o_ref):
    o_ref[0:16] = p_ref[:, :, 0:32, :].astype(F32)
    for extra in range(o_ref.shape[0] - 16):
        for part in range(2):
            for core in range(2):
                o_ref[16 + extra, part, 16 * core : 16 * core + 16, :] = p_ref[
                    2 * extra + part, core, 32:48, :
                ].astype(F32)


def out_call(pieces, mode_rows):
    return pl.pallas_call(
        out_kernel,
        in_specs=[vmem()],
        out_specs=vmem(),
        out_shape=jax.ShapeDtypeStruct((mode_rows, 2, 32, 256), F32),
        compiler_params=pltpu.CompilerParams(vmem_limit_bytes=SOLVE_LIMIT),
        name="result",
    )(pieces)


def body(
    velocity,
    adj_temp,
    radial_div,
    reciprocal_distance,
    radial_basis,
    radial_eig,
    axial_diff,
    axial_basis,
    axial_eig,
):
    row_total = lax.axis_size("row")
    col_total = lax.axis_size("col")
    row_place = lax.axis_index("row")
    col_place = lax.axis_index("col")
    chip = col_place // 2
    core = col_place % 2
    mode_rows = radial_basis.shape[0]
    circle = velocity.shape[1] * row_total
    exchange = functools.partial(lax.all_to_all, split_axis=0, concat_axis=0, tiled=True)

    fields = exchange(flux_call(velocity, adj_temp, radial_div), "row")

    def pick(array, index):
        return lax.dynamic_index_in_dim(array, index, 0, keepdims=False)

    table = azimuth_table(mode_rows * row_total, circle, circle)
    recip_half = lax.dynamic_slice_in_dim(reciprocal_distance, (row_place % 2) * 128, 128)
    basis_turned = axial_basis.T
    basis_half = pick(
        axial_basis.reshape(col_total, 2, 16, axial_basis.shape[1]).swapaxes(0, 1), core
    ).reshape(col_total * 16, axial_basis.shape[1])
    shared_mode = 16 + jnp.minimum(chip, 2 * (mode_rows - 16) - 1) // 2
    mu = axial_eig[None, :]
    whole_basis, shared_basis = pick(radial_basis, chip), pick(radial_basis, shared_mode)
    whole_eig, shared_eig = pick(radial_eig, chip)[None, :], pick(radial_eig, shared_mode)[None, :]

    later = [basis_turned, basis_half, whole_basis, shared_basis, whole_eig, shared_eig]
    fields, later = lax.optimization_barrier((fields, later))
    basis_turned, basis_half, whole_basis, shared_basis, whole_eig, shared_eig = later
    spectra = spectra_call(fields, table, recip_half[None, :])
    lines = exchange(spectra.reshape(row_total * col_total, 24, 128), ("row", "col"))
    lines = lines.reshape(row_total, col_total, 24, 128)

    own = lines[:, :, 16:24, :]
    other = lax.ppermute(own, "col", [(i, i ^ 1) for i in range(col_total)])
    whole = whole_call(
        lines, axial_diff, basis_turned, axial_basis, whole_basis, whole_eig, mu
    )
    pieces = shared_call(
        core.reshape(1), own, other, whole, axial_diff, basis_turned, basis_half,
        shared_basis, shared_eig, mu,
    )
    pieces = exchange(pieces, "col")
    return out_call(pieces.reshape(16, 2, 48, 256), mode_rows)


def solution(mesh):
    in_specs = (
        P(None, "row", "col", None),
        P("row", "col", None),
        P(),
        P(),
        P("row", None, None),
        P("row", None),
        P(),
        P(),
        P(),
    )
    out_specs = P("row", None, "col", None)
    return jax.shard_map(body, mesh=mesh, in_specs=in_specs, out_specs=out_specs, check_vma=False)
```

```python
import functools
import math

import jax
import jax.numpy as jnp
import ml_dtypes
import numpy as np
from jax import lax
from jax.experimental import pallas as pl
from jax.experimental.pallas import tpu as pltpu
from jax.sharding import PartitionSpec as P

HEAT_OFFSET = 1.0
BF = jnp.bfloat16
F32 = jnp.float32
NT_DIMS = (((1,), (1,)), ((), ()))
MIB = 1024 * 1024
SPECTRA_LIMIT = 24 * MIB
FLUX_LIMIT = 60 * MIB
SOLVE_LIMIT = 24 * MIB


def azimuth_table(mode_count, angle_count, circle):
    mode_ids = np.arange(mode_count, dtype=np.int32)
    angle_ids = np.arange(angle_count, dtype=np.int32)
    phase_index = mode_ids[:, None] * angle_ids[None, :] % circle
    angle_value = phase_index.astype(np.float32) * np.float32(2.0 * math.pi / circle)
    norm_factor = np.float32(1.0 / math.sqrt(circle))
    return np.concatenate(
        [np.cos(angle_value) * norm_factor, -np.sin(angle_value) * norm_factor], axis=0
    ).astype(ml_dtypes.bfloat16)


def smem():
    return pl.BlockSpec(memory_space=pltpu.SMEM)


def vmem():
    return pl.BlockSpec(memory_space=pltpu.VMEM)


def flux_kernel(
    chip_ref, extra_ref, v_ref, t_ref, d_ref, basis_ref, x_ref, whole_ref, shared_ref, sems
):
    t_rows, z_rows, r_rows = t_ref.shape
    temp = t_ref[...].astype(F32)
    part = pl.program_id(0)
    picks = [
        pltpu.make_async_copy(basis_ref.at[index[0]], to, sems.at[k])
        for k, (index, to) in enumerate(((chip_ref, whole_ref), (extra_ref, shared_ref)))
    ]

    @pl.when(part == 0)
    def _():
        for pick in picks:
            pick.start()

    def put(field, value):
        value = jnp.swapaxes(value, 0, 1).astype(BF)
        for group in range(4):
            for half in range(2):
                x_ref[group * 2 + half, field, 0] = value[
                    group * 8 : group * 8 + 8, :, half * 128 : half * 128 + 128
                ]

    put(1, v_ref[1].astype(F32) * temp)
    put(2, v_ref[2].astype(F32) * temp)
    radial = (v_ref[0].astype(F32) * temp).astype(BF).reshape(t_rows * z_rows, r_rows)
    div = lax.dot_general(radial, d_ref[...], NT_DIMS, preferred_element_type=F32)
    put(0, HEAT_OFFSET * temp + div.reshape(t_rows, z_rows, r_rows))

    @pl.when(part == pl.num_programs(0) - 1)
    def _():
        for pick in picks:
            pick.wait()


def flux_call(chip, extra, velocity, adj_temp, radial_div, basis):
    _, nt, nz, nr = velocity.shape
    step = 32
    anywhere = pl.BlockSpec(memory_space=pl.ANY)
    matrix = jax.ShapeDtypeStruct(basis.shape[1:], BF)
    return pl.pallas_call(
        flux_kernel,
        grid=(nt // step,),
        in_specs=[
            smem(),
            smem(),
            pl.BlockSpec((3, step, nz, nr), lambda i: (0, i, 0, 0)),
            pl.BlockSpec((step, nz, nr), lambda i: (i, 0, 0)),
            pl.BlockSpec((nr, nr), lambda i: (0, 0)),
            anywhere,
        ],
        out_specs=[
            pl.BlockSpec((8, 3, 1, 8, step, 128), lambda i: (0, 0, i, 0, 0, 0)),
            anywhere,
            anywhere,
        ],
        out_shape=[jax.ShapeDtypeStruct((8, 3, nt // step, 8, step, 128), BF), matrix, matrix],
        scratch_shapes=[pltpu.SemaphoreType.DMA((2,))],
        compiler_params=pltpu.CompilerParams(vmem_limit_bytes=FLUX_LIMIT),
        name="flux",
    )(chip, extra, velocity, adj_temp, radial_div, basis)


def spectra_kernel(half_ref, x_ref, w_ref, recip_ref, y_ref, u_ref):
    rows = w_ref.shape[0]
    modes = rows // 2
    table = w_ref[...]
    mode_id = lax.broadcasted_iota(jnp.int32, (modes, 128), 0).astype(F32)
    scale = mode_id * jnp.where(half_ref[0] == 0, recip_ref[:, :128], recip_ref[:, 128:])
    scale = jnp.concatenate([scale, scale], axis=0)
    scale = jnp.concatenate([scale, scale], axis=1)
    for z in range(0, 8, 2):

        def transform(field):
            columns = [
                jnp.concatenate(
                    [x_ref[s, field, h, z + k] for s in range(8) for h in range(2)], axis=0
                )
                for k in range(2)
            ]
            return jnp.dot(
                table, jnp.concatenate(columns, axis=1), preferred_element_type=F32
            )

        angular = transform(1).astype(BF).astype(F32)
        turned = jnp.concatenate([-angular[modes:], angular[:modes]], axis=0)
        source = transform(0) + scale * turned
        axial = transform(2)
        for k in range(2):
            lanes = slice(k * 128, k * 128 + 128)
            u_ref[pl.ds(z + k, rows, stride=16), :] = source[:, lanes]
            u_ref[pl.ds(8 + z + k, rows, stride=16), :] = axial[:, lanes]
    block = modes // 8
    for row in range(8):
        for part in range(2):
            first = (part * modes + row * block) * 16
            mine = u_ref[first : first + 16 * 16, :].reshape(16, 16, 128)
            y_ref[row, :, part, 0:16, :] = mine.astype(BF)
            for extra in range(block - 16):
                at = first + (16 + extra) * 16
                for core in range(2):
                    y_ref[row, 2 * extra + part, core, 16:24, :] = u_ref[
                        at + 8 * core : at + 8 * core + 8, :
                    ].astype(BF)
        for chip in range(2 * (block - 16), 16):
            y_ref[row, chip, :, 16:24, :] = jnp.zeros((2, 8, 128), BF)


def spectra_call(half, fields, table, recip):
    return pl.pallas_call(
        spectra_kernel,
        in_specs=[smem()] + [vmem()] * 3,
        out_specs=vmem(),
        out_shape=jax.ShapeDtypeStruct((8, 16, 2, 24, 128), BF),
        scratch_shapes=[pltpu.VMEM((table.shape[0] * 16 + 16, 128), F32)],
        compiler_params=pltpu.CompilerParams(vmem_limit_bytes=SPECTRA_LIMIT),
        name="spectra",
    )(half, fields, table, recip)


def axial_solve(hs_ref, hf_ref, low_ref, a_ref, b_ref, out_basis, r_ref, eig_ref, index, mu_ref, put, out_rows):
    nz = hs_ref.shape[0]
    lines = hs_ref.shape[1]
    tile = 512
    flux = hf_ref[...].astype(BF)
    eig = jnp.broadcast_to(eig_ref[pl.ds(index, 1), :], (8, lines))
    shift = jnp.transpose(eig)[:, 0:1] + HEAT_OFFSET
    for at in range(0, nz, tile):
        combined = hs_ref[at : at + tile, :] + jnp.dot(
            a_ref[at : at + tile, :], flux, preferred_element_type=F32
        )
        low_ref[at : at + tile, :] = combined.astype(BF)
    turned = jnp.transpose(low_ref[...])
    coefficients = []
    for at in range(0, nz, tile):
        coefficient = jnp.dot(turned, b_ref[:, at : at + tile], preferred_element_type=F32)
        coefficient = coefficient / (shift + mu_ref[:, at : at + tile])
        coefficients.append(coefficient.astype(BF))
    coefficients = jnp.concatenate(coefficients, axis=1)
    for at in range(0, out_rows, tile):
        returned = lax.dot_general(
            out_basis(at, tile), coefficients, NT_DIMS, preferred_element_type=F32
        )
        value = lax.dot_general(
            returned.astype(BF), r_ref[...], NT_DIMS, preferred_element_type=F32
        )
        put(at, tile, value.astype(BF))


def whole_kernel(
    chip_ref, y_ref, a_ref, b_ref, r_ref, eig_ref, mu_ref, o_ref, hs_ref, hf_ref, low_ref
):
    hs4 = hs_ref.reshape(32, 4, 8, 256)
    hf4 = hf_ref.reshape(32, 4, 8, 256)
    for group in range(4):
        left = jnp.concatenate(
            [y_ref[2 * group + half, :, 0:16, :].reshape(512, 128) for half in range(2)], axis=1
        )
        hat = jnp.dot(left, r_ref[...], preferred_element_type=F32).reshape(32, 2, 8, 256)
        hs4[:, group] = hat[:, 0]
        hf4[:, group] = hat[:, 1]

    def put(at, tile, value):
        o_ref[at // 32 : (at + tile) // 32] = value.reshape(tile // 32, 32, 256)

    axial_solve(
        hs_ref, hf_ref, low_ref, a_ref, b_ref, lambda at, tile: b_ref[at : at + tile, :],
        r_ref, eig_ref, chip_ref[0], mu_ref, put, 1024,
    )


def shared_kernel(
    core_ref, extra_ref, own_ref, other_ref, whole_ref, a_ref, b_ref, r_ref, eig_ref, mu_ref,
    o_ref, hs_ref, hf_ref, low_ref,
):
    first = core_ref[0] == 0
    hs4 = hs_ref.reshape(32, 4, 8, 256)
    hf4 = hf_ref.reshape(32, 4, 8, 256)
    for group in range(4):

        def hat(ref):
            left = jnp.concatenate(
                [ref[2 * group + half].astype(F32).reshape(256, 128) for half in range(2)], axis=1
            )
            return jnp.dot(
                left.astype(BF), r_ref[...], preferred_element_type=F32
            ).reshape(32, 8, 256)

        own = hat(own_ref)
        other = hat(other_ref)
        hs4[:, group] = jnp.where(first, own, other)
        hf4[:, group] = jnp.where(first, other, own)
    o_ref[:, 0:32, :] = whole_ref[...]

    def put(at, tile, value):
        o_ref[at // 16 : (at + tile) // 16, 32:48, :] = value.reshape(tile // 16, 16, 256)

    b4 = b_ref.reshape(32, 2, 16, 1024)

    def out_basis(at, tile):
        return b4[at // 16 : (at + tile) // 16, core_ref[0]].reshape(tile, 1024)

    axial_solve(
        hs_ref, hf_ref, low_ref, a_ref, b_ref, out_basis,
        r_ref, eig_ref, extra_ref[0], mu_ref, put, 512,
    )


def solve_scratch():
    return [
        pltpu.VMEM((1024, 256), F32),
        pltpu.VMEM((1024, 256), F32),
        pltpu.VMEM((1024, 256), BF),
    ]


def whole_call(chip, lines, a, b, r, eig, mu):
    return pl.pallas_call(
        whole_kernel,
        in_specs=[smem()] + [vmem()] * 6,
        out_specs=vmem(),
        out_shape=jax.ShapeDtypeStruct((32, 32, 256), BF),
        scratch_shapes=solve_scratch(),
        compiler_params=pltpu.CompilerParams(vmem_limit_bytes=SOLVE_LIMIT),
        cost_estimate=pl.CostEstimate(flops=4 * 10**9, bytes_accessed=8 * 10**6, transcendentals=0),
        name="whole_pair",
    )(chip, lines, a, b, r, eig, mu)


def shared_call(core, extra, own, other, whole, a, b, r, eig, mu):
    return pl.pallas_call(
        shared_kernel,
        in_specs=[smem()] * 2 + [vmem()] * 8,
        out_specs=vmem(),
        out_shape=jax.ShapeDtypeStruct((32, 48, 256), BF),
        scratch_shapes=solve_scratch(),
        compiler_params=pltpu.CompilerParams(vmem_limit_bytes=SOLVE_LIMIT),
        name="shared_pair",
    )(core, extra, own, other, whole, a, b, r, eig, mu)


def out_kernel(p_ref, o_ref):
    o_ref[0:16] = p_ref[:, :, 0:32, :].astype(F32)
    for extra in range(o_ref.shape[0] - 16):
        for part in range(2):
            for core in range(2):
                o_ref[16 + extra, part, 16 * core : 16 * core + 16, :] = p_ref[
                    2 * extra + part, core, 32:48, :
                ].astype(F32)


def out_call(pieces, mode_rows):
    return pl.pallas_call(
        out_kernel,
        in_specs=[vmem()],
        out_specs=vmem(),
        out_shape=jax.ShapeDtypeStruct((mode_rows, 2, 32, 256), F32),
        compiler_params=pltpu.CompilerParams(vmem_limit_bytes=SOLVE_LIMIT),
        name="result",
    )(pieces)


def body(
    velocity,
    adj_temp,
    radial_div,
    reciprocal_distance,
    radial_basis,
    radial_eig,
    axial_diff,
    axial_basis,
    axial_eig,
):
    row_total = lax.axis_size("row")
    col_total = lax.axis_size("col")
    row_place = lax.axis_index("row")
    col_place = lax.axis_index("col")
    chip = col_place // 2
    core = col_place % 2
    mode_rows = radial_basis.shape[0]
    circle = velocity.shape[1] * row_total
    exchange = functools.partial(lax.all_to_all, split_axis=0, concat_axis=0, tiled=True)

    table = jnp.asarray(azimuth_table(mode_rows * row_total, circle, circle))
    extra = (16 + jnp.minimum(chip, 2 * (mode_rows - 16) - 1) // 2).reshape(1)
    core, half, chip = core.reshape(1), (row_place % 2).reshape(1), chip.reshape(1)
    fields, whole_basis, shared_basis = flux_call(
        chip, extra, velocity, adj_temp, radial_div, radial_basis
    )
    fields, core, half, table = lax.optimization_barrier((fields, core, half, table))
    fields = exchange(fields, "row")
    mu = axial_eig[None, :]
    spectra = spectra_call(half, fields, table, reciprocal_distance[None, :])
    lines = exchange(spectra.reshape(row_total * col_total, 24, 128), ("row", "col"))
    lines = lines.reshape(row_total, col_total, 24, 128)

    own = lines[:, :, 16:24, :]
    other = lax.ppermute(own, "col", [(i, i ^ 1) for i in range(col_total)])
    whole = whole_call(chip, lines, axial_diff, axial_basis, whole_basis, radial_eig, mu)
    pieces = shared_call(
        core, extra, own, other, whole, axial_diff, axial_basis, shared_basis, radial_eig, mu
    )
    pieces = exchange(pieces, "col")
    return out_call(pieces.reshape(16, 2, 48, 256), mode_rows)


def solution(mesh):
    in_specs = (
        P(None, "row", "col", None),
        P("row", "col", None),
        P(),
        P(),
        P("row", None, None),
        P("row", None),
        P(),
        P(),
        P(),
    )
    out_specs = P("row", None, "col", None)
    return jax.shard_map(body, mesh=mesh, in_specs=in_specs, out_specs=out_specs, check_vma=False)
```

```python
import functools
import math

import jax
import jax.numpy as jnp
from jax import lax
from jax.experimental import pallas as pl
from jax.experimental.pallas import tpu as pltpu
from jax.sharding import PartitionSpec as P

HEAT_OFFSET = 1.0
BF = jnp.bfloat16
F32 = jnp.float32
NT_DIMS = (((1,), (1,)), ((), ()))
MIB = 1024 * 1024
SPECTRA_LIMIT = 24 * MIB
SOLVE_LIMIT = 24 * MIB


def azimuth_table(mode_count, angle_count, circle):
    mode_ids = jnp.arange(mode_count, dtype=jnp.int32)
    angle_ids = jnp.arange(angle_count, dtype=jnp.int32)
    phase_index = mode_ids[:, None] * angle_ids[None, :] % circle
    angle_value = phase_index.astype(F32) * (2.0 * math.pi / circle)
    norm_factor = 1.0 / math.sqrt(circle)
    return jnp.concatenate(
        [jnp.cos(angle_value) * norm_factor, -jnp.sin(angle_value) * norm_factor], axis=0
    ).astype(BF)


def vmem():
    return pl.BlockSpec(memory_space=pltpu.VMEM)


def flux_kernel(v_ref, t_ref, d_ref, x_ref):
    t_rows, z_rows, r_rows = t_ref.shape
    temp = t_ref[...].astype(F32)

    def put(field, value):
        value = jnp.swapaxes(value, 0, 1).astype(BF)
        for group in range(4):
            for half in range(2):
                x_ref[half * 4 + group, field, 0] = value[
                    group * 8 : group * 8 + 8, :, half * 128 : half * 128 + 128
                ]

    put(1, v_ref[1].astype(F32) * temp)
    put(2, v_ref[2].astype(F32) * temp)
    radial = (v_ref[0].astype(F32) * temp).astype(BF).reshape(t_rows * z_rows, r_rows)
    div = lax.dot_general(radial, d_ref[...], NT_DIMS, preferred_element_type=F32)
    put(0, HEAT_OFFSET * temp + div.reshape(t_rows, z_rows, r_rows))


def flux_call(velocity, adj_temp, radial_div):
    _, nt, nz, nr = velocity.shape
    step = 32
    return pl.pallas_call(
        flux_kernel,
        grid=(nt // step,),
        in_specs=[
            pl.BlockSpec((3, step, nz, nr), lambda i: (0, i, 0, 0)),
            pl.BlockSpec((step, nz, nr), lambda i: (i, 0, 0)),
            pl.BlockSpec((nr, nr), lambda i: (0, 0)),
        ],
        out_specs=pl.BlockSpec((8, 3, 1, 8, step, 128), lambda i: (0, 0, i, 0, 0, 0)),
        out_shape=jax.ShapeDtypeStruct((8, 3, nt // step, 8, step, 128), BF),
        compiler_params=pltpu.CompilerParams(vmem_limit_bytes=60 * MIB),
        name="flux",
    )(velocity, adj_temp, radial_div)


def spectra_kernel(x_ref, w_ref, recip_ref, y_ref, u_ref):
    rows = w_ref.shape[0]
    modes = rows // 2
    table = w_ref[...]
    mode_id = lax.broadcasted_iota(jnp.int32, (modes, 128), 0).astype(F32)
    scale = mode_id * recip_ref[...]
    scale = jnp.concatenate([scale, scale], axis=0)
    scale = jnp.concatenate([scale, scale], axis=1)
    for z in range(0, 8, 2):

        def transform(field):
            columns = [
                jnp.concatenate(
                    [
                        x_ref[s % 2 * 4 + s // 2, field, h, z + k]
                        for s in range(8)
                        for h in range(2)
                    ],
                    axis=0,
                )
                for k in range(2)
            ]
            return jnp.dot(
                table, jnp.concatenate(columns, axis=1), preferred_element_type=F32
            )

        angular = transform(1).astype(BF).astype(F32)
        turned = jnp.concatenate([-angular[modes:], angular[:modes]], axis=0)
        source = transform(0) + scale * turned
        axial = transform(2)
        for k in range(2):
            lanes = slice(k * 128, k * 128 + 128)
            u_ref[pl.ds(z + k, rows, stride=16), :] = source[:, lanes]
            u_ref[pl.ds(8 + z + k, rows, stride=16), :] = axial[:, lanes]
    block = modes // 8
    for row in range(8):
        for part in range(2):
            first = (part * modes + row * block) * 16
            mine = u_ref[first : first + 16 * 16, :].reshape(16, 16, 128)
            y_ref[row, :, part, 0:16, :] = mine.astype(BF)
            for extra in range(block - 16):
                at = first + (16 + extra) * 16
                for core in range(2):
                    y_ref[row, 2 * extra + part, core, 16:24, :] = u_ref[
                        at + 8 * core : at + 8 * core + 8, :
                    ].astype(BF)
        for chip in range(2 * (block - 16), 16):
            y_ref[row, chip, :, 16:24, :] = jnp.zeros((2, 8, 128), BF)


def spectra_call(fields, table, recip_half):
    return pl.pallas_call(
        spectra_kernel,
        in_specs=[vmem()] * 3,
        out_specs=vmem(),
        out_shape=jax.ShapeDtypeStruct((8, 16, 2, 24, 128), BF),
        scratch_shapes=[pltpu.VMEM((table.shape[0] * 16 + 16, 128), F32)],
        compiler_params=pltpu.CompilerParams(vmem_limit_bytes=SPECTRA_LIMIT),
        name="spectra",
    )(fields, table, recip_half)


def axial_solve(hs_ref, hf_ref, low_ref, a_ref, bt_ref, b_ref, r_ref, lam_ref, mu_ref, put):
    nz = hs_ref.shape[0]
    tile = 512
    flux = hf_ref[...].astype(BF)
    shift = jnp.transpose(jnp.broadcast_to(mu_ref[...], (8, nz)))[:, 0:1] + HEAT_OFFSET
    for at in range(0, nz, tile):
        combined = hs_ref[at : at + tile, :] + jnp.dot(
            a_ref[at : at + tile, :], flux, preferred_element_type=F32
        )
        low_ref[at : at + tile, :] = combined.astype(BF)
    combined = low_ref[...]
    coefficients = []
    for at in range(0, nz, tile):
        coefficient = jnp.dot(bt_ref[at : at + tile, :], combined, preferred_element_type=F32)
        coefficient = coefficient / (lam_ref[...] + shift[at : at + tile, :])
        coefficients.append(coefficient.astype(BF))
    coefficients = jnp.concatenate(coefficients, axis=0)
    out_rows = b_ref.shape[0]
    for at in range(0, out_rows, tile):
        returned = jnp.dot(b_ref[at : at + tile, :], coefficients, preferred_element_type=F32)
        value = lax.dot_general(
            returned.astype(BF), r_ref[...], NT_DIMS, preferred_element_type=F32
        )
        put(at, tile, value.astype(BF))


def whole_kernel(y_ref, a_ref, bt_ref, b_ref, r_ref, lam_ref, mu_ref, o_ref, hs_ref, hf_ref, low_ref):
    slots = o_ref.reshape(4, 4, 2, 32, 256)
    hs4 = hs_ref.reshape(32, 4, 8, 256)
    hf4 = hf_ref.reshape(32, 4, 8, 256)
    for group in range(4):
        left = jnp.concatenate(
            [y_ref[2 * group + half, :, 0:16, :].reshape(512, 128) for half in range(2)], axis=1
        )
        hat = jnp.dot(left, r_ref[...], preferred_element_type=F32).reshape(32, 2, 8, 256)
        hs4[:, group] = hat[:, 0]
        hf4[:, group] = hat[:, 1]

    def put(at, tile, value):
        value = value.reshape(tile // 256, 4, 2, 32, 256)
        for x in range(tile // 256):
            slots[:, at // 256 + x] = value[x]

    axial_solve(hs_ref, hf_ref, low_ref, a_ref, bt_ref, b_ref, r_ref, lam_ref, mu_ref, put)


def shared_kernel(
    core_ref, own_ref, other_ref, whole_ref, a_ref, bt_ref, b_ref, r_ref, lam_ref, mu_ref,
    o_ref, hs_ref, hf_ref, low_ref,
):
    first = core_ref[0] == 0
    slots = o_ref.reshape(4, 4, 2, 48, 256)
    hs4 = hs_ref.reshape(32, 4, 8, 256)
    hf4 = hf_ref.reshape(32, 4, 8, 256)
    for group in range(4):

        def hat(ref):
            left = jnp.concatenate(
                [ref[2 * group + half].astype(F32).reshape(256, 128) for half in range(2)], axis=1
            )
            return jnp.dot(
                left.astype(BF), r_ref[...], preferred_element_type=F32
            ).reshape(32, 8, 256)

        own = hat(own_ref)
        other = hat(other_ref)
        hs4[:, group] = jnp.where(first, own, other)
        hf4[:, group] = jnp.where(first, other, own)
    o_ref[:, 0:32, :] = whole_ref[...]

    def put(at, tile, value):
        value = value.reshape(tile // 128, 4, 2, 16, 256)
        for x in range(tile // 128):
            slots[:, at // 128 + x, :, 32:48, :] = value[x]

    axial_solve(hs_ref, hf_ref, low_ref, a_ref, bt_ref, b_ref, r_ref, lam_ref, mu_ref, put)


def solve_scratch():
    return [
        pltpu.VMEM((1024, 256), F32),
        pltpu.VMEM((1024, 256), F32),
        pltpu.VMEM((1024, 256), BF),
    ]


def whole_call(lines, a, bt, b, r, lam, mu):
    return pl.pallas_call(
        whole_kernel,
        in_specs=[vmem()] * 7,
        out_specs=vmem(),
        out_shape=jax.ShapeDtypeStruct((32, 32, 256), BF),
        scratch_shapes=solve_scratch(),
        compiler_params=pltpu.CompilerParams(vmem_limit_bytes=SOLVE_LIMIT),
        cost_estimate=pl.CostEstimate(flops=4 * 10**9, bytes_accessed=8 * 10**6, transcendentals=0),
        name="whole_pair",
    )(lines, a, bt, b, r, lam, mu)


def shared_call(core, own, other, whole, a, bt, b, r, lam, mu):
    return pl.pallas_call(
        shared_kernel,
        in_specs=[pl.BlockSpec(memory_space=pltpu.SMEM)] + [vmem()] * 9,
        out_specs=vmem(),
        out_shape=jax.ShapeDtypeStruct((32, 48, 256), BF),
        scratch_shapes=solve_scratch(),
        compiler_params=pltpu.CompilerParams(vmem_limit_bytes=SOLVE_LIMIT),
        name="shared_pair",
    )(core, own, other, whole, a, bt, b, r, lam, mu)


def out_kernel(p_ref, o_ref):
    for x in range(4):
        o_ref[4 * x : 4 * x + 4] = p_ref[:, x, :, 0:32, :].astype(F32)
    for extra in range(o_ref.shape[0] - 16):
        for part in range(2):
            chip = 2 * extra + part
            for core in range(2):
                o_ref[16 + extra, part, 16 * core : 16 * core + 16, :] = p_ref[
                    chip % 4, chip // 4, core, 32:48, :
                ].astype(F32)


def out_call(pieces, mode_rows):
    return pl.pallas_call(
        out_kernel,
        in_specs=[vmem()],
        out_specs=vmem(),
        out_shape=jax.ShapeDtypeStruct((mode_rows, 2, 32, 256), F32),
        compiler_params=pltpu.CompilerParams(vmem_limit_bytes=SOLVE_LIMIT),
        name="result",
    )(pieces)


def body(
    velocity,
    adj_temp,
    radial_div,
    reciprocal_distance,
    radial_basis,
    radial_eig,
    axial_diff,
    axial_basis,
    axial_eig,
):
    row_total = lax.axis_size("row")
    col_total = lax.axis_size("col")
    row_place = lax.axis_index("row")
    col_place = lax.axis_index("col")
    chip = col_place // 2
    core = col_place % 2
    mode_rows = radial_basis.shape[0]
    circle = velocity.shape[1] * row_total
    exchange = functools.partial(lax.all_to_all, split_axis=0, concat_axis=0, tiled=True)

    row_order = [[y * 2 + low for low in range(2) for y in range(4)]]
    col_order = [[x * 8 + z * 2 + c for z in range(4) for x in range(4) for c in range(2)]]
    fields = exchange(
        flux_call(velocity, adj_temp, radial_div), "row", axis_index_groups=row_order
    )

    def pick(array, index):
        return lax.dynamic_index_in_dim(array, index, 0, keepdims=False)

    table = azimuth_table(mode_rows * row_total, circle, circle)
    recip_half = lax.dynamic_slice_in_dim(reciprocal_distance, (row_place % 2) * 128, 128)
    basis_turned = axial_basis.T
    basis_half = pick(
        axial_basis.reshape(col_total, 2, 16, axial_basis.shape[1]).swapaxes(0, 1), core
    ).reshape(col_total * 16, axial_basis.shape[1])
    shared_mode = 16 + jnp.minimum(chip, 2 * (mode_rows - 16) - 1) // 2
    mu = axial_eig[None, :]
    whole_basis, shared_basis = pick(radial_basis, chip), pick(radial_basis, shared_mode)
    whole_eig, shared_eig = pick(radial_eig, chip)[None, :], pick(radial_eig, shared_mode)[None, :]

    later = [basis_turned, basis_half, whole_basis, shared_basis, whole_eig, shared_eig]
    fields, later = lax.optimization_barrier((fields, later))
    basis_turned, basis_half, whole_basis, shared_basis, whole_eig, shared_eig = later
    spectra = spectra_call(fields, table, recip_half[None, :])
    lines = exchange(spectra.reshape(row_total * col_total, 24, 128), ("row", "col"))
    lines = lines.reshape(row_total, col_total, 24, 128)

    own = lines[:, :, 16:24, :]
    other = lax.ppermute(own, "col", [(i, i ^ 1) for i in range(col_total)])
    whole = whole_call(
        lines, axial_diff, basis_turned, axial_basis, whole_basis, whole_eig, mu
    )
    pieces = shared_call(
        core.reshape(1), own, other, whole, axial_diff, basis_turned, basis_half,
        shared_basis, shared_eig, mu,
    )
    pieces = exchange(pieces, "col", axis_index_groups=col_order)
    return out_call(pieces.reshape(4, 4, 2, 48, 256), mode_rows)


def solution(mesh):
    in_specs = (
        P(None, "row", "col", None),
        P("row", "col", None),
        P(),
        P(),
        P("row", None, None),
        P("row", None),
        P(),
        P(),
        P(),
    )
    out_specs = P("row", None, "col", None)
    return jax.shard_map(body, mesh=mesh, in_specs=in_specs, out_specs=out_specs, check_vma=False)
```

```python
import functools
import math

import jax
import jax.numpy as jnp
from jax import lax
from jax.experimental import pallas as pl
from jax.experimental.pallas import tpu as pltpu
from jax.sharding import PartitionSpec as P

HEAT_OFFSET = 1.0
BF = jnp.bfloat16
F32 = jnp.float32
NT_DIMS = (((1,), (1,)), ((), ()))
MIB = 1024 * 1024
SPECTRA_LIMIT = 24 * MIB
SOLVE_LIMIT = 24 * MIB


def azimuth_table(mode_count, angle_count, circle):
    mode_ids = jnp.arange(mode_count, dtype=jnp.int32)
    angle_ids = jnp.arange(angle_count, dtype=jnp.int32)
    phase_index = mode_ids[:, None] * angle_ids[None, :] % circle
    angle_value = phase_index.astype(F32) * (2.0 * math.pi / circle)
    norm_factor = 1.0 / math.sqrt(circle)
    return jnp.concatenate(
        [jnp.cos(angle_value) * norm_factor, -jnp.sin(angle_value) * norm_factor], axis=0
    ).astype(BF)


def vmem():
    return pl.BlockSpec(memory_space=pltpu.VMEM)


def flux_kernel(v_ref, t_ref, d_ref, x_ref):
    t_rows, z_rows, r_rows = t_ref.shape
    temp = t_ref[...].astype(F32)

    def put(field, value):
        value = jnp.swapaxes(value, 0, 1).astype(BF)
        for group in range(4):
            for half in range(2):
                x_ref[half * 4 + group, field, 0] = value[
                    group * 8 : group * 8 + 8, :, half * 128 : half * 128 + 128
                ]

    put(1, v_ref[1].astype(F32) * temp)
    put(2, v_ref[2].astype(F32) * temp)
    radial = (v_ref[0].astype(F32) * temp).astype(BF).reshape(t_rows * z_rows, r_rows)
    div = lax.dot_general(radial, d_ref[...], NT_DIMS, preferred_element_type=F32)
    put(0, HEAT_OFFSET * temp + div.reshape(t_rows, z_rows, r_rows))


def flux_call(velocity, adj_temp, radial_div):
    _, nt, nz, nr = velocity.shape
    step = 32
    return pl.pallas_call(
        flux_kernel,
        grid=(nt // step,),
        in_specs=[
            pl.BlockSpec((3, step, nz, nr), lambda i: (0, i, 0, 0)),
            pl.BlockSpec((step, nz, nr), lambda i: (i, 0, 0)),
            pl.BlockSpec((nr, nr), lambda i: (0, 0)),
        ],
        out_specs=pl.BlockSpec((8, 3, 1, 8, step, 128), lambda i: (0, 0, i, 0, 0, 0)),
        out_shape=jax.ShapeDtypeStruct((8, 3, nt // step, 8, step, 128), BF),
        compiler_params=pltpu.CompilerParams(vmem_limit_bytes=60 * MIB),
        name="flux",
    )(velocity, adj_temp, radial_div)


def spectra_kernel(x_ref, w_ref, recip_ref, y_ref, u_ref):
    rows = w_ref.shape[0]
    modes = rows // 2
    table = w_ref[...]
    mode_id = lax.broadcasted_iota(jnp.int32, (modes, 128), 0).astype(F32)
    scale = mode_id * recip_ref[...]
    scale = jnp.concatenate([scale, scale], axis=0)
    scale = jnp.concatenate([scale] * 4, axis=1)
    for z in range(0, 8, 4):

        def transform(field):
            columns = [
                jnp.concatenate(
                    [
                        x_ref[s % 2 * 4 + s // 2, field, h, z + k]
                        for s in range(8)
                        for h in range(2)
                    ],
                    axis=0,
                )
                for k in range(4)
            ]
            return jnp.dot(
                table, jnp.concatenate(columns, axis=1), preferred_element_type=F32
            )

        angular = transform(1).astype(BF).astype(F32)
        turned = jnp.concatenate([-angular[modes:], angular[:modes]], axis=0)
        source = transform(0) + scale * turned
        axial = transform(2)
        for k in range(4):
            lanes = slice(k * 128, k * 128 + 128)
            u_ref[pl.ds(z + k, rows, stride=16), :] = source[:, lanes]
            u_ref[pl.ds(8 + z + k, rows, stride=16), :] = axial[:, lanes]
    block = modes // 8
    for row in range(8):
        for part in range(2):
            first = (part * modes + row * block) * 16
            mine = u_ref[first : first + 16 * 16, :].reshape(16, 16, 128)
            y_ref[row, :, part, 0:16, :] = mine.astype(BF)
            for extra in range(block - 16):
                at = first + (16 + extra) * 16
                for core in range(2):
                    y_ref[row, 2 * extra + part, core, 16:24, :] = u_ref[
                        at + 8 * core : at + 8 * core + 8, :
                    ].astype(BF)
        for chip in range(2 * (block - 16), 16):
            y_ref[row, chip, :, 16:24, :] = jnp.zeros((2, 8, 128), BF)


def spectra_call(fields, table, recip_half):
    return pl.pallas_call(
        spectra_kernel,
        in_specs=[vmem()] * 3,
        out_specs=vmem(),
        out_shape=jax.ShapeDtypeStruct((8, 16, 2, 24, 128), BF),
        scratch_shapes=[pltpu.VMEM((table.shape[0] * 16 + 16, 128), F32)],
        compiler_params=pltpu.CompilerParams(vmem_limit_bytes=SPECTRA_LIMIT),
        name="spectra",
    )(fields, table, recip_half)


def axial_solve(hs_ref, hf_ref, low_ref, a_ref, bt_ref, b_ref, r_ref, lam_ref, mu_ref, put):
    nz = hs_ref.shape[0]
    tile = 512
    flux = hf_ref[...].astype(BF)
    shift = jnp.transpose(jnp.broadcast_to(mu_ref[...], (8, nz)))[:, 0:1] + HEAT_OFFSET
    for at in range(0, nz, tile):
        combined = hs_ref[at : at + tile, :] + jnp.dot(
            a_ref[at : at + tile, :], flux, preferred_element_type=F32
        )
        low_ref[at : at + tile, :] = combined.astype(BF)
    combined = low_ref[...]
    coefficients = []
    for at in range(0, nz, tile):
        coefficient = jnp.dot(bt_ref[at : at + tile, :], combined, preferred_element_type=F32)
        coefficient = coefficient / (lam_ref[...] + shift[at : at + tile, :])
        coefficients.append(coefficient.astype(BF))
    coefficients = jnp.concatenate(coefficients, axis=0)
    out_rows = b_ref.shape[0]
    for at in range(0, out_rows, tile):
        returned = jnp.dot(b_ref[at : at + tile, :], coefficients, preferred_element_type=F32)
        value = lax.dot_general(
            returned.astype(BF), r_ref[...], NT_DIMS, preferred_element_type=F32
        )
        put(at, tile, value.astype(BF))


def whole_kernel(y_ref, a_ref, bt_ref, b_ref, r_ref, lam_ref, mu_ref, o_ref, hs_ref, hf_ref, low_ref):
    slots = o_ref.reshape(4, 4, 2, 32, 256)
    hs4 = hs_ref.reshape(32, 4, 8, 256)
    hf4 = hf_ref.reshape(32, 4, 8, 256)
    for group in range(4):
        left = jnp.concatenate(
            [y_ref[2 * group + half, :, 0:16, :].reshape(512, 128) for half in range(2)], axis=1
        )
        hat = jnp.dot(left, r_ref[...], preferred_element_type=F32).reshape(32, 2, 8, 256)
        hs4[:, group] = hat[:, 0]
        hf4[:, group] = hat[:, 1]

    def put(at, tile, value):
        value = value.reshape(tile // 256, 4, 2, 32, 256)
        for x in range(tile // 256):
            slots[:, at // 256 + x] = value[x]

    axial_solve(hs_ref, hf_ref, low_ref, a_ref, bt_ref, b_ref, r_ref, lam_ref, mu_ref, put)


def shared_kernel(
    core_ref, own_ref, other_ref, whole_ref, a_ref, bt_ref, b_ref, r_ref, lam_ref, mu_ref,
    o_ref, hs_ref, hf_ref, low_ref,
):
    first = core_ref[0] == 0
    slots = o_ref.reshape(4, 4, 2, 48, 256)
    hs4 = hs_ref.reshape(32, 4, 8, 256)
    hf4 = hf_ref.reshape(32, 4, 8, 256)
    for group in range(4):

        def hat(ref):
            left = jnp.concatenate(
                [ref[2 * group + half].astype(F32).reshape(256, 128) for half in range(2)], axis=1
            )
            return jnp.dot(
                left.astype(BF), r_ref[...], preferred_element_type=F32
            ).reshape(32, 8, 256)

        own = hat(own_ref)
        other = hat(other_ref)
        hs4[:, group] = jnp.where(first, own, other)
        hf4[:, group] = jnp.where(first, other, own)
    o_ref[:, 0:32, :] = whole_ref[...]

    def put(at, tile, value):
        value = value.reshape(tile // 128, 4, 2, 16, 256)
        for x in range(tile // 128):
            slots[:, at // 128 + x, :, 32:48, :] = value[x]

    axial_solve(hs_ref, hf_ref, low_ref, a_ref, bt_ref, b_ref, r_ref, lam_ref, mu_ref, put)


def solve_scratch():
    return [
        pltpu.VMEM((1024, 256), F32),
        pltpu.VMEM((1024, 256), F32),
        pltpu.VMEM((1024, 256), BF),
    ]


def whole_call(lines, a, bt, b, r, lam, mu):
    return pl.pallas_call(
        whole_kernel,
        in_specs=[vmem()] * 7,
        out_specs=vmem(),
        out_shape=jax.ShapeDtypeStruct((32, 32, 256), BF),
        scratch_shapes=solve_scratch(),
        compiler_params=pltpu.CompilerParams(vmem_limit_bytes=SOLVE_LIMIT),
        cost_estimate=pl.CostEstimate(flops=4 * 10**9, bytes_accessed=8 * 10**6, transcendentals=0),
        name="whole_pair",
    )(lines, a, bt, b, r, lam, mu)


def shared_call(core, own, other, whole, a, bt, b, r, lam, mu):
    return pl.pallas_call(
        shared_kernel,
        in_specs=[pl.BlockSpec(memory_space=pltpu.SMEM)] + [vmem()] * 9,
        out_specs=vmem(),
        out_shape=jax.ShapeDtypeStruct((32, 48, 256), BF),
        scratch_shapes=solve_scratch(),
        compiler_params=pltpu.CompilerParams(vmem_limit_bytes=SOLVE_LIMIT),
        name="shared_pair",
    )(core, own, other, whole, a, bt, b, r, lam, mu)


def out_kernel(p_ref, o_ref):
    for x in range(4):
        o_ref[4 * x : 4 * x + 4] = p_ref[:, x, :, 0:32, :].astype(F32)
    for extra in range(o_ref.shape[0] - 16):
        for part in range(2):
            chip = 2 * extra + part
            for core in range(2):
                o_ref[16 + extra, part, 16 * core : 16 * core + 16, :] = p_ref[
                    chip % 4, chip // 4, core, 32:48, :
                ].astype(F32)


def out_call(pieces, mode_rows):
    return pl.pallas_call(
        out_kernel,
        in_specs=[vmem()],
        out_specs=vmem(),
        out_shape=jax.ShapeDtypeStruct((mode_rows, 2, 32, 256), F32),
        compiler_params=pltpu.CompilerParams(vmem_limit_bytes=SOLVE_LIMIT),
        name="result",
    )(pieces)


def body(
    velocity,
    adj_temp,
    radial_div,
    reciprocal_distance,
    radial_basis,
    radial_eig,
    axial_diff,
    axial_basis,
    axial_eig,
):
    row_total = lax.axis_size("row")
    col_total = lax.axis_size("col")
    row_place = lax.axis_index("row")
    col_place = lax.axis_index("col")
    chip = col_place // 2
    core = col_place % 2
    mode_rows = radial_basis.shape[0]
    circle = velocity.shape[1] * row_total
    exchange = functools.partial(lax.all_to_all, split_axis=0, concat_axis=0, tiled=True)

    row_order = [[y * 2 + low for low in range(2) for y in range(4)]]
    col_order = [[x * 8 + z * 2 + c for z in range(4) for x in range(4) for c in range(2)]]
    fields = exchange(
        flux_call(velocity, adj_temp, radial_div), "row", axis_index_groups=row_order
    )

    def pick(array, index):
        return lax.dynamic_index_in_dim(array, index, 0, keepdims=False)

    table = azimuth_table(mode_rows * row_total, circle, circle)
    recip_half = lax.dynamic_slice_in_dim(reciprocal_distance, (row_place % 2) * 128, 128)
    basis_turned = axial_basis.T
    basis_half = pick(
        axial_basis.reshape(col_total, 2, 16, axial_basis.shape[1]).swapaxes(0, 1), core
    ).reshape(col_total * 16, axial_basis.shape[1])
    shared_mode = 16 + jnp.minimum(chip, 2 * (mode_rows - 16) - 1) // 2
    mu = axial_eig[None, :]
    whole_basis, shared_basis = pick(radial_basis, chip), pick(radial_basis, shared_mode)
    whole_eig, shared_eig = pick(radial_eig, chip)[None, :], pick(radial_eig, shared_mode)[None, :]

    later = [basis_turned, basis_half, whole_basis, shared_basis, whole_eig, shared_eig]
    fields, later = lax.optimization_barrier((fields, later))
    basis_turned, basis_half, whole_basis, shared_basis, whole_eig, shared_eig = later
    spectra = spectra_call(fields, table, recip_half[None, :])
    lines = exchange(spectra.reshape(row_total * col_total, 24, 128), ("row", "col"))
    lines = lines.reshape(row_total, col_total, 24, 128)

    own = lines[:, :, 16:24, :]
    other = lax.ppermute(own, "col", [(i, i ^ 1) for i in range(col_total)])
    whole = whole_call(
        lines, axial_diff, basis_turned, axial_basis, whole_basis, whole_eig, mu
    )
    pieces = shared_call(
        core.reshape(1), own, other, whole, axial_diff, basis_turned, basis_half,
        shared_basis, shared_eig, mu,
    )
    pieces = exchange(pieces, "col", axis_index_groups=col_order)
    return out_call(pieces.reshape(4, 4, 2, 48, 256), mode_rows)


def solution(mesh):
    in_specs = (
        P(None, "row", "col", None),
        P("row", "col", None),
        P(),
        P(),
        P("row", None, None),
        P("row", None),
        P(),
        P(),
        P(),
    )
    out_specs = P("row", None, "col", None)
    return jax.shard_map(body, mesh=mesh, in_specs=in_specs, out_specs=out_specs, check_vma=False)
```

```python
import functools
import math

import jax
import jax.numpy as jnp
from jax import lax
from jax.experimental import pallas as pl
from jax.experimental.pallas import tpu as pltpu
from jax.sharding import PartitionSpec as P

HEAT_OFFSET = 1.0
BF = jnp.bfloat16
F32 = jnp.float32
NT_DIMS = (((1,), (1,)), ((), ()))
MIB = 1024 * 1024
SPECTRA_LIMIT = 24 * MIB
SOLVE_LIMIT = 24 * MIB


def azimuth_table(mode_count, angle_count, circle):
    mode_ids = jnp.arange(mode_count, dtype=jnp.int32)
    angle_ids = jnp.arange(angle_count, dtype=jnp.int32)
    phase_index = mode_ids[:, None] * angle_ids[None, :] % circle
    angle_value = phase_index.astype(F32) * (2.0 * math.pi / circle)
    norm_factor = 1.0 / math.sqrt(circle)
    return jnp.concatenate(
        [jnp.cos(angle_value) * norm_factor, -jnp.sin(angle_value) * norm_factor], axis=0
    ).astype(BF)


def vmem():
    return pl.BlockSpec(memory_space=pltpu.VMEM)


def flux_kernel(v_ref, t_ref, d_ref, x_ref):
    t_rows, z_rows, r_rows = t_ref.shape
    temp = t_ref[...].astype(F32)

    def put(field, value):
        value = jnp.swapaxes(value, 0, 1).astype(BF)
        for group in range(4):
            for half in range(2):
                x_ref[half * 4 + group, field, 0] = value[
                    group * 8 : group * 8 + 8, :, half * 128 : half * 128 + 128
                ]

    put(1, v_ref[1].astype(F32) * temp)
    put(2, v_ref[2].astype(F32) * temp)
    radial = (v_ref[0].astype(F32) * temp).astype(BF).reshape(t_rows * z_rows, r_rows)
    div = lax.dot_general(radial, d_ref[...], NT_DIMS, preferred_element_type=F32)
    put(0, HEAT_OFFSET * temp + div.reshape(t_rows, z_rows, r_rows))


def flux_call(velocity, adj_temp, radial_div):
    _, nt, nz, nr = velocity.shape
    step = 32
    return pl.pallas_call(
        flux_kernel,
        grid=(nt // step,),
        in_specs=[
            pl.BlockSpec((3, step, nz, nr), lambda i: (0, i, 0, 0)),
            pl.BlockSpec((step, nz, nr), lambda i: (i, 0, 0)),
            pl.BlockSpec((nr, nr), lambda i: (0, 0)),
        ],
        out_specs=pl.BlockSpec((8, 3, 1, 8, step, 128), lambda i: (0, 0, i, 0, 0, 0)),
        out_shape=jax.ShapeDtypeStruct((8, 3, nt // step, 8, step, 128), BF),
        compiler_params=pltpu.CompilerParams(vmem_limit_bytes=60 * MIB),
        name="flux",
    )(velocity, adj_temp, radial_div)


def spectra_kernel(x_ref, w_ref, recip_ref, y_ref, u_ref):
    rows = w_ref.shape[0]
    modes = rows // 2
    table = w_ref[...]
    mode_id = lax.broadcasted_iota(jnp.int32, (modes, 128), 0).astype(F32)
    scale = mode_id * recip_ref[...]
    scale = jnp.concatenate([scale, scale], axis=0)
    scale = jnp.concatenate([scale] * 4, axis=1)
    for z in range(0, 8, 4):

        def transform(field):
            columns = [
                jnp.concatenate(
                    [
                        x_ref[s % 2 * 4 + s // 2, field, h, z + k]
                        for s in range(8)
                        for h in range(2)
                    ],
                    axis=0,
                )
                for k in range(4)
            ]
            return jnp.dot(
                table, jnp.concatenate(columns, axis=1), preferred_element_type=F32
            )

        angular = transform(1).astype(BF).astype(F32)
        turned = jnp.concatenate([-angular[modes:], angular[:modes]], axis=0)
        source = transform(0) + scale * turned
        axial = transform(2)
        for k in range(4):
            lanes = slice(k * 128, k * 128 + 128)
            u_ref[pl.ds(z + k, rows, stride=16), :] = source[:, lanes]
            u_ref[pl.ds(8 + z + k, rows, stride=16), :] = axial[:, lanes]
    block = modes // 8
    for row in range(8):
        for part in range(2):
            first = (part * modes + row * block) * 16
            mine = u_ref[first : first + 16 * 16, :].reshape(16, 16, 128)
            y_ref[:, part, row, 0:16, :] = mine.astype(BF)
            for extra in range(block - 16):
                at = first + (16 + extra) * 16
                for core in range(2):
                    y_ref[2 * extra + part, core, row, 16:24, :] = u_ref[
                        at + 8 * core : at + 8 * core + 8, :
                    ].astype(BF)
        for chip in range(2 * (block - 16), 16):
            y_ref[chip, :, row, 16:24, :] = jnp.zeros((2, 8, 128), BF)


def spectra_call(fields, table, recip_half):
    return pl.pallas_call(
        spectra_kernel,
        in_specs=[vmem()] * 3,
        out_specs=vmem(),
        out_shape=jax.ShapeDtypeStruct((16, 2, 8, 24, 128), BF),
        scratch_shapes=[pltpu.VMEM((table.shape[0] * 16 + 16, 128), F32)],
        compiler_params=pltpu.CompilerParams(vmem_limit_bytes=SPECTRA_LIMIT),
        name="spectra",
    )(fields, table, recip_half)


def axial_solve(hs_ref, hf_ref, low_ref, a_ref, bt_ref, b_ref, r_ref, lam_ref, mu_ref, put):
    nz = hs_ref.shape[0]
    tile = 512
    flux = hf_ref[...].astype(BF)
    shift = jnp.transpose(jnp.broadcast_to(mu_ref[...], (8, nz)))[:, 0:1] + HEAT_OFFSET
    for at in range(0, nz, tile):
        combined = hs_ref[at : at + tile, :] + jnp.dot(
            a_ref[at : at + tile, :], flux, preferred_element_type=F32
        )
        low_ref[at : at + tile, :] = combined.astype(BF)
    combined = low_ref[...]
    coefficients = []
    for at in range(0, nz, tile):
        coefficient = jnp.dot(bt_ref[at : at + tile, :], combined, preferred_element_type=F32)
        coefficient = coefficient / (lam_ref[...] + shift[at : at + tile, :])
        coefficients.append(coefficient.astype(BF))
    coefficients = jnp.concatenate(coefficients, axis=0)
    out_rows = b_ref.shape[0]
    for at in range(0, out_rows, tile):
        returned = jnp.dot(b_ref[at : at + tile, :], coefficients, preferred_element_type=F32)
        value = lax.dot_general(
            returned.astype(BF), r_ref[...], NT_DIMS, preferred_element_type=F32
        )
        put(at, tile, value.astype(BF))


def whole_kernel(y_ref, a_ref, bt_ref, b_ref, r_ref, lam_ref, mu_ref, o_ref, hs_ref, hf_ref, low_ref):
    slots = o_ref.reshape(4, 4, 2, 32, 256)
    hs4 = hs_ref.reshape(32, 4, 8, 256)
    hf4 = hf_ref.reshape(32, 4, 8, 256)
    for group in range(4):
        left = jnp.concatenate(
            [y_ref[:, 2 * group + half, 0:16, :].reshape(512, 128) for half in range(2)], axis=1
        )
        hat = jnp.dot(left, r_ref[...], preferred_element_type=F32).reshape(32, 2, 8, 256)
        hs4[:, group] = hat[:, 0]
        hf4[:, group] = hat[:, 1]

    def put(at, tile, value):
        value = value.reshape(tile // 256, 4, 2, 32, 256)
        for x in range(tile // 256):
            slots[:, at // 256 + x] = value[x]

    axial_solve(hs_ref, hf_ref, low_ref, a_ref, bt_ref, b_ref, r_ref, lam_ref, mu_ref, put)


def shared_kernel(
    core_ref, own_ref, other_ref, whole_ref, a_ref, bt_ref, b_ref, r_ref, lam_ref, mu_ref,
    o_ref, hs_ref, hf_ref, low_ref,
):
    first = core_ref[0] == 0
    slots = o_ref.reshape(4, 4, 2, 48, 256)
    hs4 = hs_ref.reshape(32, 4, 8, 256)
    hf4 = hf_ref.reshape(32, 4, 8, 256)
    for group in range(4):

        def hat(ref):
            left = jnp.concatenate(
                [ref[:, 2 * group + half].astype(F32).reshape(256, 128) for half in range(2)], axis=1
            )
            return jnp.dot(
                left.astype(BF), r_ref[...], preferred_element_type=F32
            ).reshape(32, 8, 256)

        own = hat(own_ref)
        other = hat(other_ref)
        hs4[:, group] = jnp.where(first, own, other)
        hf4[:, group] = jnp.where(first, other, own)
    o_ref[:, 0:32, :] = whole_ref[...]

    def put(at, tile, value):
        value = value.reshape(tile // 128, 4, 2, 16, 256)
        for x in range(tile // 128):
            slots[:, at // 128 + x, :, 32:48, :] = value[x]

    axial_solve(hs_ref, hf_ref, low_ref, a_ref, bt_ref, b_ref, r_ref, lam_ref, mu_ref, put)


def solve_scratch():
    return [
        pltpu.VMEM((1024, 256), F32),
        pltpu.VMEM((1024, 256), F32),
        pltpu.VMEM((1024, 256), BF),
    ]


def whole_call(lines, a, bt, b, r, lam, mu):
    return pl.pallas_call(
        whole_kernel,
        in_specs=[vmem()] * 7,
        out_specs=vmem(),
        out_shape=jax.ShapeDtypeStruct((32, 32, 256), BF),
        scratch_shapes=solve_scratch(),
        compiler_params=pltpu.CompilerParams(vmem_limit_bytes=SOLVE_LIMIT),
        cost_estimate=pl.CostEstimate(flops=4 * 10**9, bytes_accessed=8 * 10**6, transcendentals=0),
        name="whole_pair",
    )(lines, a, bt, b, r, lam, mu)


def shared_call(core, own, other, whole, a, bt, b, r, lam, mu):
    return pl.pallas_call(
        shared_kernel,
        in_specs=[pl.BlockSpec(memory_space=pltpu.SMEM)] + [vmem()] * 9,
        out_specs=vmem(),
        out_shape=jax.ShapeDtypeStruct((32, 48, 256), BF),
        scratch_shapes=solve_scratch(),
        compiler_params=pltpu.CompilerParams(vmem_limit_bytes=SOLVE_LIMIT),
        name="shared_pair",
    )(core, own, other, whole, a, bt, b, r, lam, mu)


def out_kernel(p_ref, o_ref):
    for x in range(4):
        o_ref[4 * x : 4 * x + 4] = p_ref[:, x, :, 0:32, :].astype(F32)
    for extra in range(o_ref.shape[0] - 16):
        for part in range(2):
            chip = 2 * extra + part
            for core in range(2):
                o_ref[16 + extra, part, 16 * core : 16 * core + 16, :] = p_ref[
                    chip % 4, chip // 4, core, 32:48, :
                ].astype(F32)


def out_call(pieces, mode_rows):
    return pl.pallas_call(
        out_kernel,
        in_specs=[vmem()],
        out_specs=vmem(),
        out_shape=jax.ShapeDtypeStruct((mode_rows, 2, 32, 256), F32),
        compiler_params=pltpu.CompilerParams(vmem_limit_bytes=SOLVE_LIMIT),
        name="result",
    )(pieces)


def body(
    velocity,
    adj_temp,
    radial_div,
    reciprocal_distance,
    radial_basis,
    radial_eig,
    axial_diff,
    axial_basis,
    axial_eig,
):
    row_total = lax.axis_size("row")
    col_total = lax.axis_size("col")
    row_place = lax.axis_index("row")
    col_place = lax.axis_index("col")
    chip = col_place // 2
    core = col_place % 2
    mode_rows = radial_basis.shape[0]
    circle = velocity.shape[1] * row_total
    exchange = functools.partial(lax.all_to_all, split_axis=0, concat_axis=0, tiled=True)

    row_order = [[y * 2 + low for low in range(2) for y in range(4)]]
    col_order = [[x * 8 + z * 2 + c for z in range(4) for x in range(4) for c in range(2)]]
    fields = exchange(
        flux_call(velocity, adj_temp, radial_div), "row", axis_index_groups=row_order
    )

    def pick(array, index):
        return lax.dynamic_index_in_dim(array, index, 0, keepdims=False)

    table = azimuth_table(mode_rows * row_total, circle, circle)
    recip_half = lax.dynamic_slice_in_dim(reciprocal_distance, (row_place % 2) * 128, 128)
    basis_turned = axial_basis.T
    basis_half = pick(
        axial_basis.reshape(col_total, 2, 16, axial_basis.shape[1]).swapaxes(0, 1), core
    ).reshape(col_total * 16, axial_basis.shape[1])
    shared_mode = 16 + jnp.minimum(chip, 2 * (mode_rows - 16) - 1) // 2
    mu = axial_eig[None, :]
    whole_basis, shared_basis = pick(radial_basis, chip), pick(radial_basis, shared_mode)
    whole_eig, shared_eig = pick(radial_eig, chip)[None, :], pick(radial_eig, shared_mode)[None, :]

    later = [basis_turned, basis_half, whole_basis, shared_basis, whole_eig, shared_eig]
    fields, later = lax.optimization_barrier((fields, later))
    basis_turned, basis_half, whole_basis, shared_basis, whole_eig, shared_eig = later
    spectra = spectra_call(fields, table, recip_half[None, :])
    lines = exchange(spectra.reshape(row_total * col_total, 24, 128), ("col", "row"))
    lines = lines.reshape(col_total, row_total, 24, 128)

    own = lines[:, :, 16:24, :]
    other = lax.ppermute(own, "col", [(i, i ^ 1) for i in range(col_total)])
    whole = whole_call(
        lines, axial_diff, basis_turned, axial_basis, whole_basis, whole_eig, mu
    )
    pieces = shared_call(
        core.reshape(1), own, other, whole, axial_diff, basis_turned, basis_half,
        shared_basis, shared_eig, mu,
    )
    pieces = exchange(pieces, "col", axis_index_groups=col_order)
    return out_call(pieces.reshape(4, 4, 2, 48, 256), mode_rows)


def solution(mesh):
    in_specs = (
        P(None, "row", "col", None),
        P("row", "col", None),
        P(),
        P(),
        P("row", None, None),
        P("row", None),
        P(),
        P(),
        P(),
    )
    out_specs = P("row", None, "col", None)
    return jax.shard_map(body, mesh=mesh, in_specs=in_specs, out_specs=out_specs, check_vma=False)
```
